256 devices in a mesh: ifg: 16 (over z, core), strip: 16 (over y, x).
Axes of the slice: x: 4, y: 4, z: 8, core: 2. Of those that a mesh axis runs over, the one named last changes fastest.
Arguments:
- grad_x: float32 [64, 1024, 1024], P('ifg', 'strip'), may hold values from -3 to 3
- grad_y: float32 [64, 1024, 1024], P('ifg', 'strip'), may hold values from -3 to 3
- coherence: float32 [64, 1024, 1024], P('ifg', 'strip'), may hold values from 0 to 1, as said below
- pairs: int32 [64, 2], replicated, may hold values from 0 to 31, as said below
Outputs:
- unwrapped: float32 [64, 1024, 1024], P('ifg', 'strip')
- series: float32 [32, 1024, 1024], P('ifg', 'strip')
The draws below stay inside these ranges and needn't reach their ends.
Inputs may be any that keep to these rules, and one draw needn't show every extreme that they name: Every row names an earlier date first and a later date second; the pairs connect all 32 dates. `coherence`: positive weights.
All inputs are finite; a program needn't handle non-finite values.
Results may differ from the reference program's by a relative error of at most 0.0003.
Values sent between devices are 32-bit elements; how exact they have to be, the bound alone decides.
A program may use at most 64 MiB of HBM per device.

```python
import jax
import jax.numpy as jnp
from jax import lax

IFGS = 64
DATES = 32
COLS = 1024
ITERS = 3
NROWS = 1024


def draw_coherence(key, part):
    first = jax.random.fold_in(key, 0)
    rows = jnp.arange(NROWS, dtype=jnp.float32) / NROWS
    ramp = 0.33 + 0.67 * rows
    base = jax.random.uniform(first, (IFGS, NROWS, COLS), jnp.float32, 0.3, 1.0)
    return (base * ramp[None, :, None]).astype(jnp.float32)


def draw_pairs(key, part):
    key_first, key_span, key_order = jax.random.split(key, 3)
    extra = IFGS - DATES + 1
    chain_first = jnp.arange(DATES - 1, dtype=jnp.int32)
    extra_first = jax.random.randint(key_first, (extra,), 0, DATES - 1).astype(jnp.int32)
    spans = jax.random.randint(key_span, (extra,), 1, 6).astype(jnp.int32)
    extra_second = jnp.minimum(extra_first + spans, DATES - 1)
    earlier = jnp.concatenate([chain_first, extra_first])
    later = jnp.concatenate([chain_first + 1, extra_second])
    order = jax.random.permutation(key_order, IFGS)
    return jnp.stack([earlier, later], axis=1)[order].astype(jnp.int32)


def block_scale(key, dims, cuts, low, top_value):
    level = 1.0
    for dim, blocks in cuts:
        draws = jax.random.uniform(jax.random.fold_in(jax.random.fold_in(key, 6), dim), (blocks,), jnp.float32, low / len(cuts), top_value / len(cuts))
        level = level * jnp.repeat(jnp.exp(draws), dims[dim] // blocks).reshape((-1,) + (1,) * (len(dims) - 1 - dim))
    return level


def setup_inputs(seed: int = 0) -> dict:
    key_list = jax.random.split(jax.random.key(seed), 5)
    return {
        "grad_x": jnp.clip(jax.random.uniform(key_list[0], (IFGS, NROWS, COLS), jnp.float32, -3.0, 3.0) * block_scale(key_list[0], (IFGS, NROWS, COLS), ((0, 16), (1, 16)), -0.4, 0.0), -3.0, 3.0),
        "grad_y": jnp.clip(jax.random.uniform(key_list[1], (IFGS, NROWS, COLS), jnp.float32, -3.0, 3.0) * block_scale(key_list[1], (IFGS, NROWS, COLS), ((0, 16), (1, 16)), -0.4, 0.0), -3.0, 3.0),
        "coherence": draw_coherence(jax.random.fold_in(key_list[4], 71), 0),
        "pairs": draw_pairs(jax.random.fold_in(key_list[4], 71), 0),
    }


damping = 0.1

def prev_col(field):
    return jnp.pad(field, ((0, 0), (0, 0), (1, 0)))[:, :, :-1]

def prev_row(field):
    return jnp.pad(field, ((0, 0), (1, 0), (0, 0)))[:, :-1, :]

def weights_of(coherence):
    wx = jnp.pad(coherence[:, :, :-1] * coherence[:, :, 1:], ((0, 0), (0, 0), (0, 1)))
    wy = jnp.pad(coherence[:, :-1, :] * coherence[:, 1:, :], ((0, 0), (0, 1), (0, 0)))
    return (wx, wy)

def divergence(flux_x, flux_y):
    return flux_x - prev_col(flux_x) + flux_y - prev_row(flux_y)

def operate(field, wx, wy):
    diff_x = jnp.pad(field[:, :, 1:] - field[:, :, :-1], ((0, 0), (0, 0), (0, 1)))
    diff_y = jnp.pad(field[:, 1:, :] - field[:, :-1, :], ((0, 0), (0, 1), (0, 0)))
    return damping * field - divergence(wx * diff_x, wy * diff_y)

def inverse_map(pairs):
    slots = jnp.arange(DATES, dtype=jnp.int32)
    design = (pairs[:, 1:2] == slots[None, :]).astype(jnp.float32) - (pairs[:, 0:1] == slots[None, :]).astype(jnp.float32)
    normal = jnp.dot(design.T, design, precision=lax.Precision.HIGHEST) + 1.0
    factor = jnp.linalg.cholesky(normal)
    return jax.scipy.linalg.cho_solve((factor, True), design.T)

def reference(grad_x, grad_y, coherence, pairs):
    wx, wy = weights_of(coherence)
    rhs = -divergence(wx * grad_x, wy * grad_y)
    solution = jnp.zeros_like(rhs)
    residual = rhs
    direction = rhs
    norm_now = jnp.sum(residual * residual, axis=(1, 2))
    for step in range(ITERS):
        image = operate(direction, wx, wy)
        alpha = norm_now / jnp.sum(direction * image, axis=(1, 2))
        solution = solution + alpha[:, None, None] * direction
        residual = residual - alpha[:, None, None] * image
        norm_next = jnp.sum(residual * residual, axis=(1, 2))
        direction = residual + (norm_next / norm_now)[:, None, None] * direction
        norm_now = norm_next
    mapping = inverse_map(pairs)
    series = jnp.einsum('dk,krc->drc', mapping, solution, precision=lax.Precision.HIGHEST)
    return (solution, series)
```

```python
import jax
import jax.numpy as jnp
from jax import lax
from jax.experimental import pallas as pl
from jax.experimental.pallas import tpu as pltpu
from jax.sharding import PartitionSpec as P

MESH = pl.DeviceIdType.MESH
DAMPING = 0.1
DATES = 32
IFGS = 64
GROUPS = 16
STRIPS = 16
K = 4
OWN = 2
ROWS = 64
COLS = 1024
TILES = ROWS // 8
CHUNKS = 4
EPS = 3e-7


def tile(t):
    return slice(8 * t, 8 * t + 8)


def rows_iota():
    return lax.broadcasted_iota(jnp.int32, (8, COLS), 0)


def fold(field):
    total = field[:, :128]
    for c in range(1, COLS // 128):
        total = total + field[:, 128 * c : 128 * c + 128]
    return total


def next_row(now, after):
    return jnp.where(rows_iota() == 7, pltpu.roll(after, 7, 0), pltpu.roll(now, 7, 0))


def edge_x(coherence):
    lanes = lax.broadcasted_iota(jnp.int32, (8, COLS), 1)
    return jnp.where(lanes == COLS - 1, 0.0, coherence * pltpu.roll(coherence, COLS - 1, 1))


def laplace(p_ref, q_ref, wx_ref, wy_ref, i, first, last, inner):
    top = rows_iota() == 0
    now = p_ref[i, tile(first), :]
    if first > 0:
        before = p_ref[i, tile(first - 1), :]
        carry = pltpu.roll(wy_ref[i, tile(first - 1), :] * (next_row(before, now) - before), 1, 0)
    else:
        carry = jnp.zeros((8, COLS), jnp.float32)
    for t in range(first, last + 1):
        after = p_ref[i, tile(t + 1), :] if t < TILES + 1 else now
        flux_y = wy_ref[i, tile(t), :] * (next_row(now, after) - now)
        flux_x = wx_ref[i, tile(t), :] * (pltpu.roll(now, COLS - 1, 1) - now)
        turned = pltpu.roll(flux_y, 1, 0)
        out = pltpu.roll(flux_x, 1, 1) - flux_x + jnp.where(top, carry, turned) - flux_y
        q_ref[i, tile(t), :] = out
        inner(t, now, out)
        carry = turned
        now = after


def energy(p_ref, wx_ref, wy_ref, i, tiles):
    total = jnp.zeros((8, 128), jnp.float32)
    for t in tiles:
        now = p_ref[i, tile(t), :]
        diff_y = next_row(now, p_ref[i, tile(t + 1), :]) - now
        diff_x = pltpu.roll(now, COLS - 1, 1) - now
        total = total + fold(
            wy_ref[i, tile(t), :] * diff_y * diff_y + wx_ref[i, tile(t), :] * diff_x * diff_x
        )
    return total


def coefficients(m):
    a = [m[j + 1] + DAMPING * m[j] for j in range(5)]
    zero = jnp.zeros_like(m[0])
    d0 = a[0]
    good0 = d0 > 0.0
    inv0 = 1.0 / jnp.where(good0, d0, 1.0)
    l1 = a[1] * inv0
    l2 = a[2] * inv0
    d1 = a[2] - l1 * a[1]
    good1 = d1 > EPS * a[2]
    inv1 = jnp.where(good1, 1.0 / jnp.where(good1, d1, 1.0), zero)
    l3 = (a[3] - l2 * a[1]) * inv1
    d2 = a[4] - l2 * a[2] - l3 * (a[3] - l2 * a[1])
    good2 = good1 & (d2 > EPS * a[4])
    inv2 = jnp.where(good2, 1.0 / jnp.where(good2, d2, 1.0), zero)
    y1 = m[1] - l1 * m[0]
    y2 = m[2] - l2 * m[0] - l3 * y1
    c2 = y2 * inv2
    c1 = y1 * inv1 - l3 * c2
    c0 = m[0] * inv0 - l1 * c1 - l2 * c2
    return c0, c1, c2


def inverse_rows(pairs):
    lanes = lax.broadcasted_iota(jnp.int32, (IFGS, 128), 1)
    rows = lax.broadcasted_iota(jnp.int32, (IFGS, 128), 0)
    design = (pairs[:, 1:2] == lanes).astype(jnp.float32) - (pairs[:, 0:1] == lanes).astype(
        jnp.float32
    )
    both = design + (lanes - DATES == rows).astype(jnp.float32)
    table = lax.dot_general(
        design, both, (((0,), (0,)), ((), ())), precision=lax.Precision.HIGHEST,
        preferred_element_type=jnp.float32,
    )[:DATES]
    spread = lax.broadcasted_iota(jnp.int32, (DATES, 128), 1)
    level = lax.broadcasted_iota(jnp.int32, (DATES, 1), 0)
    table = table + (spread < DATES).astype(jnp.float32)
    for j in range(DATES):
        row = table[j : j + 1, :] / table[j : j + 1, j : j + 1]
        column = table[:, j : j + 1] - (level == j).astype(jnp.float32)
        table = table - column * row
    return table


def kernel(
    gx_hbm, gy_hbm, co_hbm, pairs_ref, x_hbm, series_hbm,
    gx, gy, co, wx, wy, v0, v1, v2, x, sums, moments, folded, coef, spread, phases, dates,
    load_sem, halo_send, halo_recv, sum_send, sum_recv, x_send, x_recv, s_send, s_recv, out_sem,
):
    g, s = lax.axis_index("ifg"), lax.axis_index("strip")
    z, core = g // 2, lax.rem(g, 2)
    rows = rows_iota()

    loads = []
    for i in range(K):
        for a, (src, dst, low) in enumerate(((co_hbm, co, 8), (gy_hbm, gy, 8), (gx_hbm, gx, 0))):
            loads.append(
                pltpu.make_async_copy(src.at[i], dst.at[i, low : low + ROWS], load_sem.at[i, a])
            )
    for copy in loads:
        copy.start()

    barrier = pltpu.get_barrier_semaphore()

    @pl.loop(1, STRIPS)
    def _(d):
        pl.semaphore_signal(
            barrier, inc=1, device_id=(g, lax.rem(s + d, STRIPS)), device_id_type=MESH
        )
        pl.semaphore_signal(
            barrier, inc=1, device_id=(lax.rem(g + d, GROUPS), s), device_id_type=MESH
        )

    nothing = jnp.zeros((K, 8, COLS), jnp.float32)

    @pl.when(s == 0)
    def _():
        co[:, tile(0), :] = nothing
        gy[:, tile(0), :] = nothing
        v0[:, tile(0), :] = nothing

    @pl.when(s == STRIPS - 1)
    def _():
        co[:, tile(TILES + 1), :] = nothing
        v0[:, tile(TILES + 1), :] = nothing

    for copy in loads:
        copy.wait()

    @pl.loop(0, K)
    def _(i):
        carry = jnp.zeros((8, COLS), jnp.float32)
        now = co[i, tile(1), :]
        for t in range(1, TILES + 1):
            after = co[i, tile(t + 1), :] if t < TILES else jnp.zeros((8, COLS), jnp.float32)
            weight_x = edge_x(now)
            weight_y = now * next_row(now, after)
            flux_x = weight_x * gx[i, tile(t - 1), :]
            flux_y = weight_y * gy[i, tile(t), :]
            turned = pltpu.roll(flux_y, 1, 0)
            wx[i, tile(t), :] = weight_x
            wy[i, tile(t), :] = weight_y
            v0[i, tile(t), :] = (
                pltpu.roll(flux_x, 1, 1) - flux_x + jnp.where(rows == 0, carry, turned) - flux_y
            )
            carry = turned
            now = after

    pl.semaphore_wait(barrier, STRIPS + GROUPS - 2)

    def halo(n, src, dst, low, high, shift, device):
        return pltpu.make_async_remote_copy(
            src_ref=src.at[:, low:high],
            dst_ref=dst.at[:, low + shift : high + shift],
            send_sem=halo_send.at[n],
            recv_sem=halo_recv.at[n],
            device_id=(g, device),
            device_id_type=MESH,
        )

    up = jnp.maximum(s - 1, 0)
    down = jnp.minimum(s + 1, STRIPS - 1)
    upward = [halo(0, co, co, 8, 11, ROWS, up), halo(1, v0, v0, 8, 11, ROWS, up)]
    downward = [
        halo(2, co, co, 6 + ROWS, 8 + ROWS, -ROWS, down),
        halo(3, v0, v0, 6 + ROWS, 8 + ROWS, -ROWS, down),
        halo(4, gy, gy, 7 + ROWS, 8 + ROWS, -ROWS, down),
    ]

    @pl.when(s > 0)
    def _():
        for copy in upward:
            copy.start()

    @pl.when(s < STRIPS - 1)
    def _():
        for copy in downward:
            copy.start()

    def first_pass(i, spans):
        totals = [jnp.zeros((8, 128), jnp.float32)] * 3

        def inner(t, p, q):
            if 1 <= t <= TILES:
                for n, product in enumerate((p * p, p * q, q * q)):
                    totals[n] = totals[n] + fold(product)

        for low, high in spans:
            laplace(v0, v1, wx, wy, i, low, high, inner)
        return totals

    def second_pass(i, spans):
        totals = [jnp.zeros((8, 128), jnp.float32)] * 2

        def inner(t, p, q):
            if 1 <= t <= TILES:
                for n, product in enumerate((p * q, q * q)):
                    totals[n] = totals[n] + fold(product)

        for low, high in spans:
            laplace(v1, v2, wx, wy, i, low, high, inner)
        return totals

    @pl.loop(0, K)
    def _(i):
        totals = first_pass(i, [(2, 7)]) + second_pass(i, [(3, 6)])
        totals.append(energy(v2, wx, wy, i, range(3, 6)))
        for n, total in enumerate(totals):
            sums[i, n] = total

    @pl.when(s > 0)
    def _():
        for copy in upward:
            copy.wait_send()
        for copy in downward:
            copy.wait_recv()

    @pl.when(s < STRIPS - 1)
    def _():
        for copy in downward:
            copy.wait_send()
        for copy in upward:
            copy.wait_recv()

    for i in range(K):
        low, high, beyond = co[i, tile(0), :], co[i, tile(TILES), :], co[i, tile(TILES + 1), :]
        wx[i, tile(0), :] = edge_x(low)
        wx[i, tile(TILES + 1), :] = edge_x(beyond)
        weight_low = low * next_row(low, co[i, tile(1), :])
        weight_high = high * next_row(high, beyond)
        wy[i, tile(0), :] = weight_low
        wy[i, tile(TILES), :] = weight_high
        wy[i, tile(TILES + 1), :] = beyond * next_row(beyond, beyond)
        for t, weight in ((0, weight_low), (TILES, weight_high)):
            flux = weight * gy[i, tile(t), :]
            here, there = v0[i, tile(t), :], v0[i, tile(t + 1), :]
            v0[i, tile(t), :] = jnp.where(rows == 7, here - flux, here)
            v0[i, tile(t + 1), :] = jnp.where(rows == 0, there + pltpu.roll(flux, 1, 0), there)

    @pl.loop(0, K)
    def _(i):
        totals = first_pass(i, [(0, 1), (8, 9)]) + second_pass(i, [(1, 2), (7, 9)])
        totals.append(energy(v2, wx, wy, i, (1, 2, 6, 7, 8)))
        for n, total in enumerate(totals):
            moments[s, pl.ds(K * n + i, 1), :] = jnp.sum(sums[i, n] + total, axis=0, keepdims=True)

    def share(d):
        return pltpu.make_async_remote_copy(
            src_ref=moments.at[s],
            dst_ref=moments.at[s],
            send_sem=sum_send,
            recv_sem=sum_recv,
            device_id=(g, lax.rem(s + d, STRIPS)),
            device_id_type=MESH,
        )

    @pl.loop(1, STRIPS)
    def _(d):
        share(d).start()

    table = inverse_rows(pairs_ref[...])
    for k in range(IFGS):
        spread[k] = jnp.broadcast_to(table[:, DATES + k : DATES + k + 1], (DATES, 128))

    others = moments.at[0 : STRIPS - 1]
    pltpu.make_async_copy(others, others, sum_recv).wait()
    total = moments[0]
    for d in range(1, STRIPS):
        total = total + moments[d]
    folded[...] = jnp.broadcast_to(jnp.sum(total, axis=1, keepdims=True), folded.shape)
    for j, c in enumerate(coefficients([folded[K * n : K * n + K, :] for n in range(6)])):
        coef[j] = c

    def send_x(d, q):
        t = lax.rem(g + d, GROUPS)
        row = pl.multiple_of(32 * lax.rem(t, 2) + 8 * q, 8)
        column = pl.multiple_of(128 * (t // 2), 128)
        return pltpu.make_async_remote_copy(
            src_ref=x.at[:, pl.ds(row, 8), pl.ds(column, 128)],
            dst_ref=phases.at[pl.ds(K * g, K), pl.ds(8 * q, 8)],
            send_sem=x_send.at[q],
            recv_sem=x_recv.at[q],
            device_id=(t, s),
            device_id_type=MESH,
        )

    own_column = pl.multiple_of(128 * z, 128)
    for q in range(CHUNKS):

        @pl.loop(0, K)
        def _(i):
            c0, c1, c2 = (coef[j, pl.ds(i, 1), 0:1] for j in range(3))
            for half in range(2):
                t = 4 * half + q
                x[i, tile(t), :] = (
                    c0 * v0[i, tile(t + 1), :] + c1 * v1[i, tile(t + 1), :] + c2 * v2[i, tile(t + 1), :]
                )

        @pl.loop(1, GROUPS)
        def _(d):
            send_x(d, q).start()

        own_row = pl.multiple_of(32 * core + 8 * q, 8)
        phases[pl.ds(K * g, K), tile(q), :] = x[:, pl.ds(own_row, 8), pl.ds(own_column, 128)]

    x_out = pltpu.make_async_copy(x, x_hbm, out_sem.at[CHUNKS])
    x_out.start()

    def place(q):
        row = pl.multiple_of(32 * core + 8 * q, 8)
        return series_hbm.at[:, pl.ds(row, 8), pl.ds(own_column, 128)]

    def send_s(d, q):
        t = lax.rem(g + d, GROUPS)
        return pltpu.make_async_remote_copy(
            src_ref=dates.at[pl.ds(OWN * t, OWN), tile(q)],
            dst_ref=place(q),
            send_sem=s_send.at[q],
            recv_sem=s_recv.at[q],
            device_id=(t, s),
            device_id_type=MESH,
        )

    own = []
    for q in range(CHUNKS):
        others = phases.at[0 : K * (GROUPS - 1), tile(q)]
        pltpu.make_async_copy(others, others, x_recv.at[q]).wait()

        def add(k, totals):
            phase = phases[k, tile(q), :]
            return tuple(
                total + spread[k, d : d + 1, :] * phase for d, total in enumerate(totals)
            )

        totals = lax.fori_loop(0, IFGS, add, (jnp.zeros((8, 128), jnp.float32),) * DATES)
        for d in range(DATES):
            dates[d, tile(q), :] = totals[d]

        @pl.loop(1, GROUPS)
        def _(d):
            send_s(d, q).start()

        own.append(pltpu.make_async_copy(dates.at[pl.ds(OWN * g, OWN), tile(q)], place(q), out_sem.at[q]))
        own[q].start()

    pltpu.make_async_copy(moments.at[0 : STRIPS - 1], moments.at[0 : STRIPS - 1], sum_send).wait()
    for q in range(CHUNKS):
        others = phases.at[0 : K * (GROUPS - 1), tile(q)]
        pltpu.make_async_copy(others, others, x_send.at[q]).wait()
        others = dates.at[0 : OWN * (GROUPS - 1), tile(q)]
        pltpu.make_async_copy(others, others, s_send.at[q]).wait()
        pltpu.make_async_copy(others, others, s_recv.at[q]).wait()
        own[q].wait()
    x_out.wait()


def on_device(grad_x, grad_y, coherence, pairs):
    f32 = jnp.float32
    dma = pltpu.SemaphoreType.DMA
    halo = pltpu.VMEM((K, ROWS + 16, COLS), f32)
    return pl.pallas_call(
        kernel,
        out_shape=(
            jax.ShapeDtypeStruct((K, ROWS, COLS), f32),
            jax.ShapeDtypeStruct((OWN, ROWS, COLS), f32),
        ),
        in_specs=[pl.BlockSpec(memory_space=pl.ANY)] * 3 + [pl.BlockSpec(memory_space=pltpu.VMEM)],
        out_specs=(pl.BlockSpec(memory_space=pl.ANY),) * 2,
        scratch_shapes=[
            pltpu.VMEM((K, ROWS, COLS), f32),
            halo, halo, halo, halo, halo, halo, halo,
            pltpu.VMEM((K, ROWS, COLS), f32),
            pltpu.VMEM((K, 6, 8, 128), f32),
            pltpu.VMEM((STRIPS, 6 * K, 128), f32),
            pltpu.VMEM((6 * K, 128), f32),
            pltpu.VMEM((3, K, 128), f32),
            pltpu.VMEM((IFGS, DATES, 128), f32),
            pltpu.VMEM((IFGS, 32, 128), f32),
            pltpu.VMEM((DATES, 32, 128), f32),
            dma((K, 3)), dma((5,)), dma((5,)), dma, dma,
            dma((CHUNKS,)), dma((CHUNKS,)), dma((CHUNKS,)), dma((CHUNKS,)), dma((CHUNKS + 1,)),
        ],
        compiler_params=pltpu.CompilerParams(
            collective_id=0, has_side_effects=True, vmem_limit_bytes=48 * 1024 * 1024
        ),
    )(grad_x, grad_y, coherence, pairs)


def solution(mesh):
    split = P("ifg", "strip", None)
    return jax.shard_map(
        on_device, mesh=mesh, in_specs=(split, split, split, P()), out_specs=(split, split),
        check_vma=False,
    )
```

```python
import jax
import jax.numpy as jnp
from jax import lax
from jax.experimental import pallas as pl
from jax.experimental.pallas import tpu as pltpu
from jax.sharding import PartitionSpec as P

MESH = pl.DeviceIdType.MESH
DAMPING = 0.1
DATES = 32
IFGS = 64
GROUPS = 16
STRIPS = 16
K = 4
OWN = 2
ROWS = 64
COLS = 1024
TILES = ROWS // 8
CHUNKS = 4
EPS = 3e-7


def tile(t):
    return slice(8 * t, 8 * t + 8)


def rows_iota():
    return lax.broadcasted_iota(jnp.int32, (8, COLS), 0)


def fold(field):
    total = field[:, :128]
    for c in range(1, COLS // 128):
        total = total + field[:, 128 * c : 128 * c + 128]
    return total


def next_row(now, after):
    return jnp.where(rows_iota() == 7, pltpu.roll(after, 7, 0), pltpu.roll(now, 7, 0))


def edge_x(coherence):
    lanes = lax.broadcasted_iota(jnp.int32, (8, COLS), 1)
    return jnp.where(lanes == COLS - 1, 0.0, coherence * pltpu.roll(coherence, COLS - 1, 1))


def laplace(p_ref, q_ref, wx_ref, wy_ref, i, first, last, inner):
    top = rows_iota() == 0
    now = p_ref[i, tile(first), :]
    if first > 0:
        before = p_ref[i, tile(first - 1), :]
        carry = pltpu.roll(wy_ref[i, tile(first - 1), :] * (next_row(before, now) - before), 1, 0)
    else:
        carry = jnp.zeros((8, COLS), jnp.float32)
    for t in range(first, last + 1):
        after = p_ref[i, tile(t + 1), :] if t < TILES + 1 else now
        flux_y = wy_ref[i, tile(t), :] * (next_row(now, after) - now)
        flux_x = wx_ref[i, tile(t), :] * (pltpu.roll(now, COLS - 1, 1) - now)
        turned = pltpu.roll(flux_y, 1, 0)
        out = pltpu.roll(flux_x, 1, 1) - flux_x + jnp.where(top, carry, turned) - flux_y
        q_ref[i, tile(t), :] = out
        inner(t, now, out)
        carry = turned
        now = after


def energy(p_ref, wx_ref, wy_ref, i, tiles):
    total = jnp.zeros((8, 128), jnp.float32)
    for t in tiles:
        now = p_ref[i, tile(t), :]
        diff_y = next_row(now, p_ref[i, tile(t + 1), :]) - now
        diff_x = pltpu.roll(now, COLS - 1, 1) - now
        total = total + fold(
            wy_ref[i, tile(t), :] * diff_y * diff_y + wx_ref[i, tile(t), :] * diff_x * diff_x
        )
    return total


def coefficients(m):
    a = [m[j + 1] + DAMPING * m[j] for j in range(5)]
    zero = jnp.zeros_like(m[0])
    d0 = a[0]
    good0 = d0 > 0.0
    inv0 = 1.0 / jnp.where(good0, d0, 1.0)
    l1 = a[1] * inv0
    l2 = a[2] * inv0
    d1 = a[2] - l1 * a[1]
    good1 = d1 > EPS * a[2]
    inv1 = jnp.where(good1, 1.0 / jnp.where(good1, d1, 1.0), zero)
    l3 = (a[3] - l2 * a[1]) * inv1
    d2 = a[4] - l2 * a[2] - l3 * (a[3] - l2 * a[1])
    good2 = good1 & (d2 > EPS * a[4])
    inv2 = jnp.where(good2, 1.0 / jnp.where(good2, d2, 1.0), zero)
    y1 = m[1] - l1 * m[0]
    y2 = m[2] - l2 * m[0] - l3 * y1
    c2 = y2 * inv2
    c1 = y1 * inv1 - l3 * c2
    c0 = m[0] * inv0 - l1 * c1 - l2 * c2
    return c0, c1, c2


def inverse_rows(pairs):
    date = lax.broadcasted_iota(jnp.int32, (128, IFGS), 0)
    design = (pairs[1:2, :] == date).astype(jnp.float32) - (pairs[0:1, :] == date).astype(jnp.float32)
    lanes = lax.broadcasted_iota(jnp.int32, (IFGS, 128), 1)
    shifted = lanes - DATES == lax.broadcasted_iota(jnp.int32, (IFGS, 128), 0)
    table = lax.dot_general(
        design[:DATES], design, (((1,), (1,)), ((), ())), precision=lax.Precision.HIGHEST,
        preferred_element_type=jnp.float32,
    ) + jnp.dot(
        design[:DATES], shifted.astype(jnp.float32), precision=lax.Precision.HIGHEST,
        preferred_element_type=jnp.float32,
    )
    spread = lax.broadcasted_iota(jnp.int32, (DATES, 128), 1)
    level = lax.broadcasted_iota(jnp.int32, (DATES, 1), 0)
    table = table + (spread < DATES).astype(jnp.float32)
    for j in range(DATES):
        row = table[j : j + 1, :] / table[j : j + 1, j : j + 1]
        column = table[:, j : j + 1] - (level == j).astype(jnp.float32)
        table = table - column * row
    return table


def kernel(
    gx_hbm, gy_hbm, co_hbm, pairs_hbm, x_hbm, series_hbm,
    gx, gy, co, wx, wy, v0, v1, v2, x, sums, moments, folded, coef, spread, phases, dates, pairs,
    load_sem, halo_send, halo_recv, sum_send, sum_recv, x_send, x_recv, s_send, s_recv, out_sem,
):
    g, s = lax.axis_index("ifg"), lax.axis_index("strip")
    z, core = g // 2, lax.rem(g, 2)
    rows = rows_iota()

    loads = []
    for i in range(K):
        for a, (src, dst, low) in enumerate(((co_hbm, co, 8), (gy_hbm, gy, 8), (gx_hbm, gx, 0))):
            loads.append(
                pltpu.make_async_copy(src.at[i], dst.at[i, low : low + ROWS], load_sem.at[i, a])
            )
    for copy in loads:
        copy.start()
    pairs_in = pltpu.make_async_copy(pairs_hbm, pairs, out_sem.at[CHUNKS + 1])
    pairs_in.start()

    barrier = pltpu.get_barrier_semaphore()

    @pl.loop(1, STRIPS)
    def _(d):
        pl.semaphore_signal(
            barrier, inc=1, device_id=(g, lax.rem(s + d, STRIPS)), device_id_type=MESH
        )
        pl.semaphore_signal(
            barrier, inc=1, device_id=(lax.rem(g + d, GROUPS), s), device_id_type=MESH
        )

    nothing = jnp.zeros((K, 8, COLS), jnp.float32)

    @pl.when(s == 0)
    def _():
        co[:, tile(0), :] = nothing
        gy[:, tile(0), :] = nothing
        v0[:, tile(0), :] = nothing

    @pl.when(s == STRIPS - 1)
    def _():
        co[:, tile(TILES + 1), :] = nothing
        v0[:, tile(TILES + 1), :] = nothing

    for copy in loads:
        copy.wait()

    @pl.loop(0, K)
    def _(i):
        carry = jnp.zeros((8, COLS), jnp.float32)
        now = co[i, tile(1), :]
        for t in range(1, TILES + 1):
            after = co[i, tile(t + 1), :] if t < TILES else jnp.zeros((8, COLS), jnp.float32)
            weight_x = edge_x(now)
            weight_y = now * next_row(now, after)
            flux_x = weight_x * gx[i, tile(t - 1), :]
            flux_y = weight_y * gy[i, tile(t), :]
            turned = pltpu.roll(flux_y, 1, 0)
            wx[i, tile(t), :] = weight_x
            wy[i, tile(t), :] = weight_y
            v0[i, tile(t), :] = (
                pltpu.roll(flux_x, 1, 1) - flux_x + jnp.where(rows == 0, carry, turned) - flux_y
            )
            carry = turned
            now = after

    pl.semaphore_wait(barrier, STRIPS + GROUPS - 2)

    def halo(n, src, dst, low, high, shift, device):
        return pltpu.make_async_remote_copy(
            src_ref=src.at[:, low:high],
            dst_ref=dst.at[:, low + shift : high + shift],
            send_sem=halo_send.at[n],
            recv_sem=halo_recv.at[n],
            device_id=(g, device),
            device_id_type=MESH,
        )

    up = jnp.maximum(s - 1, 0)
    down = jnp.minimum(s + 1, STRIPS - 1)
    upward = [halo(0, co, co, 8, 11, ROWS, up), halo(1, v0, v0, 8, 11, ROWS, up)]
    downward = [
        halo(2, co, co, 6 + ROWS, 8 + ROWS, -ROWS, down),
        halo(3, v0, v0, 6 + ROWS, 8 + ROWS, -ROWS, down),
        halo(4, gy, gy, 7 + ROWS, 8 + ROWS, -ROWS, down),
    ]

    @pl.when(s > 0)
    def _():
        for copy in upward:
            copy.start()

    @pl.when(s < STRIPS - 1)
    def _():
        for copy in downward:
            copy.start()

    def first_pass(i, spans):
        totals = [jnp.zeros((8, 128), jnp.float32)] * 3

        def inner(t, p, q):
            if 1 <= t <= TILES:
                for n, product in enumerate((p * p, p * q, q * q)):
                    totals[n] = totals[n] + fold(product)

        for low, high in spans:
            laplace(v0, v1, wx, wy, i, low, high, inner)
        return totals

    def second_pass(i, spans):
        totals = [jnp.zeros((8, 128), jnp.float32)] * 2

        def inner(t, p, q):
            if 1 <= t <= TILES:
                for n, product in enumerate((p * q, q * q)):
                    totals[n] = totals[n] + fold(product)

        for low, high in spans:
            laplace(v1, v2, wx, wy, i, low, high, inner)
        return totals

    @pl.loop(0, K)
    def _(i):
        totals = first_pass(i, [(2, 7)]) + second_pass(i, [(3, 6)])
        totals.append(energy(v2, wx, wy, i, range(3, 6)))
        for n, total in enumerate(totals):
            sums[i, n] = total

    @pl.when(s > 0)
    def _():
        for copy in upward:
            copy.wait_send()
        for copy in downward:
            copy.wait_recv()

    @pl.when(s < STRIPS - 1)
    def _():
        for copy in downward:
            copy.wait_send()
        for copy in upward:
            copy.wait_recv()

    for i in range(K):
        low, high, beyond = co[i, tile(0), :], co[i, tile(TILES), :], co[i, tile(TILES + 1), :]
        wx[i, tile(0), :] = edge_x(low)
        wx[i, tile(TILES + 1), :] = edge_x(beyond)
        weight_low = low * next_row(low, co[i, tile(1), :])
        weight_high = high * next_row(high, beyond)
        wy[i, tile(0), :] = weight_low
        wy[i, tile(TILES), :] = weight_high
        wy[i, tile(TILES + 1), :] = beyond * next_row(beyond, beyond)
        for t, weight in ((0, weight_low), (TILES, weight_high)):
            flux = weight * gy[i, tile(t), :]
            here, there = v0[i, tile(t), :], v0[i, tile(t + 1), :]
            v0[i, tile(t), :] = jnp.where(rows == 7, here - flux, here)
            v0[i, tile(t + 1), :] = jnp.where(rows == 0, there + pltpu.roll(flux, 1, 0), there)

    @pl.loop(0, K)
    def _(i):
        totals = first_pass(i, [(0, 1), (8, 9)]) + second_pass(i, [(1, 2), (7, 9)])
        totals.append(energy(v2, wx, wy, i, (1, 2, 6, 7, 8)))
        for n, total in enumerate(totals):
            moments[s, pl.ds(K * n + i, 1), :] = jnp.sum(sums[i, n] + total, axis=0, keepdims=True)

    def share(d):
        return pltpu.make_async_remote_copy(
            src_ref=moments.at[s],
            dst_ref=moments.at[s],
            send_sem=sum_send,
            recv_sem=sum_recv,
            device_id=(g, lax.rem(s + d, STRIPS)),
            device_id_type=MESH,
        )

    @pl.loop(1, STRIPS)
    def _(d):
        share(d).start()

    others = moments.at[0 : STRIPS - 1]
    pltpu.make_async_copy(others, others, sum_recv).wait()
    total = moments[0]
    for d in range(1, STRIPS):
        total = total + moments[d]
    folded[...] = jnp.broadcast_to(jnp.sum(total, axis=1, keepdims=True), folded.shape)
    for j, c in enumerate(coefficients([folded[K * n : K * n + K, :] for n in range(6)])):
        coef[j] = c

    def send_x(d, q):
        t = lax.rem(g + d, GROUPS)
        row = pl.multiple_of(32 * lax.rem(t, 2) + 8 * q, 8)
        column = pl.multiple_of(128 * (t // 2), 128)
        return pltpu.make_async_remote_copy(
            src_ref=x.at[:, pl.ds(row, 8), pl.ds(column, 128)],
            dst_ref=phases.at[pl.ds(K * g, K), pl.ds(8 * q, 8)],
            send_sem=x_send.at[q],
            recv_sem=x_recv.at[q],
            device_id=(t, s),
            device_id_type=MESH,
        )

    own_column = pl.multiple_of(128 * z, 128)
    for q in range(CHUNKS):

        @pl.loop(0, K)
        def _(i):
            c0, c1, c2 = (coef[j, pl.ds(i, 1), 0:1] for j in range(3))
            for half in range(2):
                t = 4 * half + q
                x[i, tile(t), :] = (
                    c0 * v0[i, tile(t + 1), :] + c1 * v1[i, tile(t + 1), :] + c2 * v2[i, tile(t + 1), :]
                )

        @pl.loop(1, GROUPS)
        def _(d):
            send_x(d, q).start()

        own_row = pl.multiple_of(32 * core + 8 * q, 8)
        phases[pl.ds(K * g, K), tile(q), :] = x[:, pl.ds(own_row, 8), pl.ds(own_column, 128)]

    x_out = pltpu.make_async_copy(x, x_hbm, out_sem.at[CHUNKS])
    x_out.start()

    pairs_in.wait()
    table = inverse_rows(pairs[...])
    for k in range(IFGS):
        spread[k] = jnp.broadcast_to(table[:, DATES + k : DATES + k + 1], (DATES, 128))

    def place(q):
        row = pl.multiple_of(32 * core + 8 * q, 8)
        return series_hbm.at[:, pl.ds(row, 8), pl.ds(own_column, 128)]

    def send_s(d, q):
        t = lax.rem(g + d, GROUPS)
        return pltpu.make_async_remote_copy(
            src_ref=dates.at[pl.ds(OWN * t, OWN), tile(q)],
            dst_ref=place(q),
            send_sem=s_send.at[q],
            recv_sem=s_recv.at[q],
            device_id=(t, s),
            device_id_type=MESH,
        )

    own = []
    for q in range(CHUNKS):
        others = phases.at[0 : K * (GROUPS - 1), tile(q)]
        pltpu.make_async_copy(others, others, x_recv.at[q]).wait()

        def add(k, totals):
            phase = phases[k, tile(q), :]
            return tuple(
                total + spread[k, d : d + 1, :] * phase for d, total in enumerate(totals)
            )

        totals = lax.fori_loop(0, IFGS, add, (jnp.zeros((8, 128), jnp.float32),) * DATES)
        for d in range(DATES):
            dates[d, tile(q), :] = totals[d]

        @pl.loop(1, GROUPS)
        def _(d):
            send_s(d, q).start()

        own.append(pltpu.make_async_copy(dates.at[pl.ds(OWN * g, OWN), tile(q)], place(q), out_sem.at[q]))
        own[q].start()

    pltpu.make_async_copy(moments.at[0 : STRIPS - 1], moments.at[0 : STRIPS - 1], sum_send).wait()
    for q in range(CHUNKS):
        others = phases.at[0 : K * (GROUPS - 1), tile(q)]
        pltpu.make_async_copy(others, others, x_send.at[q]).wait()
        others = dates.at[0 : OWN * (GROUPS - 1), tile(q)]
        pltpu.make_async_copy(others, others, s_send.at[q]).wait()
        pltpu.make_async_copy(others, others, s_recv.at[q]).wait()
        own[q].wait()
    x_out.wait()


def hand_over(x_ref, series_ref, x_out, series_out, sem):
    copies = [pltpu.make_async_copy(x_ref.at[i], x_out.at[i], sem.at[i]) for i in range(K)]
    copies += [
        pltpu.make_async_copy(series_ref.at[i], series_out.at[i], sem.at[K + i]) for i in range(OWN)
    ]
    for copy in copies:
        copy.start()
    for copy in copies:
        copy.wait()


def on_device(grad_x, grad_y, coherence, pairs):
    f32 = jnp.float32
    dma = pltpu.SemaphoreType.DMA
    halo = pltpu.VMEM((K, ROWS + 16, COLS), f32)
    phases, series = pl.pallas_call(
        kernel,
        out_shape=(
            jax.ShapeDtypeStruct((K, ROWS, COLS), f32),
            jax.ShapeDtypeStruct((OWN, ROWS, COLS), f32),
        ),
        in_specs=[pl.BlockSpec(memory_space=pl.ANY)] * 4,
        out_specs=(pl.BlockSpec(memory_space=pl.ANY),) * 2,
        scratch_shapes=[
            pltpu.VMEM((K, ROWS, COLS), f32),
            halo, halo, halo, halo, halo, halo, halo,
            pltpu.VMEM((K, ROWS, COLS), f32),
            pltpu.VMEM((K, 6, 8, 128), f32),
            pltpu.VMEM((STRIPS, 6 * K, 128), f32),
            pltpu.VMEM((6 * K, 128), f32),
            pltpu.VMEM((3, K, 128), f32),
            pltpu.VMEM((IFGS, DATES, 128), f32),
            pltpu.VMEM((IFGS, 32, 128), f32),
            pltpu.VMEM((DATES, 32, 128), f32),
            pltpu.VMEM((2, IFGS), jnp.int32),
            dma((K, 3)), dma((5,)), dma((5,)), dma, dma,
            dma((CHUNKS,)), dma((CHUNKS,)), dma((CHUNKS,)), dma((CHUNKS,)), dma((CHUNKS + 2,)),
        ],
        compiler_params=pltpu.CompilerParams(
            collective_id=0, has_side_effects=True, vmem_limit_bytes=52 * 1024 * 1024
        ),
    )(grad_x, grad_y, coherence, pairs.T)
    return pl.pallas_call(
        hand_over,
        out_shape=(
            jax.ShapeDtypeStruct((K, ROWS, COLS), f32),
            jax.ShapeDtypeStruct((OWN, ROWS, COLS), f32),
        ),
        in_specs=[pl.BlockSpec(memory_space=pltpu.VMEM)] * 2,
        out_specs=(pl.BlockSpec(memory_space=pl.ANY),) * 2,
        scratch_shapes=[dma((K + OWN,))],
        compiler_params=pltpu.CompilerParams(vmem_limit_bytes=4 * 1024 * 1024),
    )(phases, series)


def solution(mesh):
    split = P("ifg", "strip", None)
    return jax.shard_map(
        on_device, mesh=mesh, in_specs=(split, split, split, P()), out_specs=(split, split),
        check_vma=False,
    )
```

```python
import jax
import jax.numpy as jnp
from jax import lax
from jax.experimental import pallas as pl
from jax.experimental.pallas import tpu as pltpu
from jax.sharding import PartitionSpec as P

MESH = pl.DeviceIdType.MESH
DAMPING = 0.1
DATES = 32
IFGS = 64
GROUPS = 16
STRIPS = 16
K = 4
PAIR = 2
OWN = 2
ROWS = 64
COLS = 1024
TILES = ROWS // 8
CHUNKS = 4
EPS = 3e-7
PEERS = [(dz, other) for dz in (4, 3, 5, 2, 6, 1, 7) for other in (0, 1)] + [(0, 1)]


def tile(t):
    return slice(8 * t, 8 * t + 8)


def rows_iota():
    return lax.broadcasted_iota(jnp.int32, (8, COLS), 0)


def fold(field):
    total = field[:, :128]
    for c in range(1, COLS // 128):
        total = total + field[:, 128 * c : 128 * c + 128]
    return total


def next_row(now, after):
    return jnp.where(rows_iota() == 7, pltpu.roll(after, 7, 0), pltpu.roll(now, 7, 0))


def edge_x(coherence):
    lanes = lax.broadcasted_iota(jnp.int32, (8, COLS), 1)
    return jnp.where(lanes == COLS - 1, 0.0, coherence * pltpu.roll(coherence, COLS - 1, 1))


def laplace(p_ref, q_ref, wx_ref, wy_ref, i, first, last, inner):
    top = rows_iota() == 0
    now = p_ref[i, tile(first), :]
    if first > 0:
        before = p_ref[i, tile(first - 1), :]
        carry = pltpu.roll(wy_ref[i, tile(first - 1), :] * (next_row(before, now) - before), 1, 0)
    else:
        carry = jnp.zeros((8, COLS), jnp.float32)
    for t in range(first, last + 1):
        after = p_ref[i, tile(t + 1), :] if t < TILES + 1 else now
        flux_y = wy_ref[i, tile(t), :] * (next_row(now, after) - now)
        flux_x = wx_ref[i, tile(t), :] * (pltpu.roll(now, COLS - 1, 1) - now)
        turned = pltpu.roll(flux_y, 1, 0)
        out = pltpu.roll(flux_x, 1, 1) - flux_x + jnp.where(top, carry, turned) - flux_y
        q_ref[i, tile(t), :] = out
        inner(t, now, out)
        carry = turned
        now = after


def energy(p_ref, wx_ref, wy_ref, i, tiles):
    total = jnp.zeros((8, 128), jnp.float32)
    for t in tiles:
        now = p_ref[i, tile(t), :]
        diff_y = next_row(now, p_ref[i, tile(t + 1), :]) - now
        diff_x = pltpu.roll(now, COLS - 1, 1) - now
        total = total + fold(
            wy_ref[i, tile(t), :] * diff_y * diff_y + wx_ref[i, tile(t), :] * diff_x * diff_x
        )
    return total


def coefficients(m):
    a = [m[j + 1] + DAMPING * m[j] for j in range(5)]
    zero = jnp.zeros_like(m[0])
    d0 = a[0]
    good0 = d0 > 0.0
    inv0 = 1.0 / jnp.where(good0, d0, 1.0)
    l1 = a[1] * inv0
    l2 = a[2] * inv0
    d1 = a[2] - l1 * a[1]
    good1 = d1 > EPS * a[2]
    inv1 = jnp.where(good1, 1.0 / jnp.where(good1, d1, 1.0), zero)
    l3 = (a[3] - l2 * a[1]) * inv1
    d2 = a[4] - l2 * a[2] - l3 * (a[3] - l2 * a[1])
    good2 = good1 & (d2 > EPS * a[4])
    inv2 = jnp.where(good2, 1.0 / jnp.where(good2, d2, 1.0), zero)
    y1 = m[1] - l1 * m[0]
    y2 = m[2] - l2 * m[0] - l3 * y1
    c2 = y2 * inv2
    c1 = y1 * inv1 - l3 * c2
    c0 = m[0] * inv0 - l1 * c1 - l2 * c2
    return c0, c1, c2


def inverse_rows(pairs):
    date = lax.broadcasted_iota(jnp.int32, (128, IFGS), 0)
    design = (pairs[1:2, :] == date).astype(jnp.float32) - (pairs[0:1, :] == date).astype(jnp.float32)
    lanes = lax.broadcasted_iota(jnp.int32, (IFGS, 128), 1)
    shifted = lanes - DATES == lax.broadcasted_iota(jnp.int32, (IFGS, 128), 0)
    table = lax.dot_general(
        design[:DATES], design, (((1,), (1,)), ((), ())), precision=lax.Precision.HIGHEST,
        preferred_element_type=jnp.float32,
    ) + jnp.dot(
        design[:DATES], shifted.astype(jnp.float32), precision=lax.Precision.HIGHEST,
        preferred_element_type=jnp.float32,
    )
    spread = lax.broadcasted_iota(jnp.int32, (DATES, 128), 1)
    level = lax.broadcasted_iota(jnp.int32, (DATES, 1), 0)
    table = table + (spread < DATES).astype(jnp.float32)
    for j in range(DATES):
        row = table[j : j + 1, :] / table[j : j + 1, j : j + 1]
        column = table[:, j : j + 1] - (level == j).astype(jnp.float32)
        table = table - column * row
    return table


def kernel(
    gx_hbm, gy_hbm, co_hbm, pairs_hbm, x_hbm, series_hbm,
    gx, gy, co, wx, wy, basis, x, sums, moments, coef, spread, phases, early, factors, dates, pairs,
    load_sem, halo_send, halo_recv, sum_send, sum_recv, early_send, early_recv, c_send, c_recv,
    x_send, x_recv, s_send, s_recv, x_out, own_out, pairs_sem,
):
    g, s = lax.axis_index("ifg"), lax.axis_index("strip")
    z, core = g // 2, lax.rem(g, 2)
    rows = rows_iota()
    lane = lax.broadcasted_iota(jnp.int32, (1, 128), 1)
    v0, v1, v2 = (basis.at[j] for j in range(3))

    def load(n, a):
        src, dst, low = ((co_hbm, co, 8), (gy_hbm, gy, 8), (gx_hbm, gx, 0))[a]
        first, last = ((0, 16), (48, 64), (16, 48))[n]
        return pltpu.make_async_copy(
            src.at[:, first:last], dst.at[:, low + first : low + last], load_sem.at[n, a]
        )

    for n in range(3):
        for a in range(3):
            load(n, a).start()
    pairs_in = pltpu.make_async_copy(pairs_hbm, pairs, pairs_sem)
    pairs_in.start()

    barrier = pltpu.get_barrier_semaphore()

    @pl.loop(1, STRIPS)
    def _(d):
        pl.semaphore_signal(
            barrier, inc=1, device_id=(g, lax.rem(s + d, STRIPS)), device_id_type=MESH
        )
        pl.semaphore_signal(
            barrier, inc=1, device_id=(lax.rem(g + d, GROUPS), s), device_id_type=MESH
        )

    nothing = jnp.zeros((K, 8, COLS), jnp.float32)

    @pl.when(s == 0)
    def _():
        co[:, tile(0), :] = nothing
        gy[:, tile(0), :] = nothing
        v0[:, tile(0), :] = nothing

    @pl.when(s == STRIPS - 1)
    def _():
        co[:, tile(TILES + 1), :] = nothing
        v0[:, tile(TILES + 1), :] = nothing

    def right_side(i, first, last):
        now = co[i, tile(first), :]
        if first > 1:
            before = co[i, tile(first - 1), :]
            carry = pltpu.roll(before * next_row(before, now) * gy[i, tile(first - 1), :], 1, 0)
        else:
            carry = jnp.zeros((8, COLS), jnp.float32)
        for t in range(first, last + 1):
            after = co[i, tile(t + 1), :] if t < TILES else jnp.zeros((8, COLS), jnp.float32)
            weight_x = edge_x(now)
            weight_y = now * next_row(now, after)
            flux_x = weight_x * gx[i, tile(t - 1), :]
            flux_y = weight_y * gy[i, tile(t), :]
            turned = pltpu.roll(flux_y, 1, 0)
            wx[i, tile(t), :] = weight_x
            wy[i, tile(t), :] = weight_y
            v0[i, tile(t), :] = (
                pltpu.roll(flux_x, 1, 1) - flux_x + jnp.where(rows == 0, carry, turned) - flux_y
            )
            carry = turned
            now = after

    for n in range(2):
        for a in range(3):
            load(n, a).wait()

    @pl.loop(0, K)
    def _(i):
        right_side(i, 1, 1)
        right_side(i, TILES, TILES)

    pl.semaphore_wait(barrier, STRIPS + GROUPS - 2)

    up = jnp.maximum(s - 1, 0)
    down = jnp.minimum(s + 1, STRIPS - 1)

    def halo(i, n, src, low, high, shift, device):
        return pltpu.make_async_remote_copy(
            src_ref=src.at[PAIR * i : PAIR * i + PAIR, low:high],
            dst_ref=src.at[PAIR * i : PAIR * i + PAIR, low + shift : high + shift],
            send_sem=halo_send.at[i, n],
            recv_sem=halo_recv.at[i, n],
            device_id=(g, device),
            device_id_type=MESH,
        )

    def upward(i):
        return [halo(i, 0, co, 8, 11, ROWS, up), halo(i, 1, v0, 8, 11, ROWS, up)]

    def downward(i):
        return [
            halo(i, 2, co, 6 + ROWS, 8 + ROWS, -ROWS, down),
            halo(i, 3, v0, 6 + ROWS, 8 + ROWS, -ROWS, down),
            halo(i, 4, gy, 7 + ROWS, 8 + ROWS, -ROWS, down),
        ]

    for i in range(K // PAIR):

        @pl.when(s > 0)
        def _():
            for copy in upward(i):
                copy.start()

        @pl.when(s < STRIPS - 1)
        def _():
            for copy in downward(i):
                copy.start()

    def first_pass(i, spans):
        totals = [jnp.zeros((8, 128), jnp.float32)] * 3

        def inner(t, p, q):
            if 1 <= t <= TILES:
                for n, product in enumerate((p * p, p * q, q * q)):
                    totals[n] = totals[n] + fold(product)

        for low, high in spans:
            laplace(v0, v1, wx, wy, i, low, high, inner)
        return totals

    def second_pass(i, spans):
        totals = [jnp.zeros((8, 128), jnp.float32)] * 2

        def inner(t, p, q):
            if 1 <= t <= TILES:
                for n, product in enumerate((p * q, q * q)):
                    totals[n] = totals[n] + fold(product)

        for low, high in spans:
            laplace(v1, v2, wx, wy, i, low, high, inner)
        return totals

    def interior(i):
        totals = first_pass(i, [(2, 7)]) + second_pass(i, [(3, 6)])
        totals.append(energy(v2, wx, wy, i, range(3, 6)))
        for n, total in enumerate(totals):
            sums[i, n] = total

    def target(offset):
        dz, other = offset
        there, half = lax.rem(z + dz, GROUPS // 2), lax.rem(core + other, 2)
        return 2 * there + half, half, pl.multiple_of(128 * there, 128)

    def send_early(d):
        t, half, column = target(d)
        row = pl.multiple_of(8 + 16 + 16 * half, 8)
        return pltpu.make_async_remote_copy(
            src_ref=basis.at[:, K - 1, pl.ds(row, 16), pl.ds(column, 128)],
            dst_ref=early.at[g],
            send_sem=early_send,
            recv_sem=early_recv,
            device_id=(t, s),
            device_id_type=MESH,
        )

    for a in range(3):
        load(2, a).wait()
    right_side(K - 1, 2, TILES - 1)
    interior(K - 1)

    for offset in PEERS:
        send_early(offset).start()

    @pl.loop(0, K - 1)
    def _(i):
        right_side(i, 2, TILES - 1)
        interior(i)

    def share(i, d):
        return pltpu.make_async_remote_copy(
            src_ref=moments.at[i, s],
            dst_ref=moments.at[i, s],
            send_sem=sum_send.at[i],
            recv_sem=sum_recv.at[i],
            device_id=(g, lax.rem(s + d, STRIPS)),
            device_id_type=MESH,
        )

    def ends(i, pair):
        low, high, beyond = co[i, tile(0), :], co[i, tile(TILES), :], co[i, tile(TILES + 1), :]
        wx[i, tile(0), :] = edge_x(low)
        wx[i, tile(TILES + 1), :] = edge_x(beyond)
        weight_low = low * next_row(low, co[i, tile(1), :])
        weight_high = high * next_row(high, beyond)
        wy[i, tile(0), :] = weight_low
        wy[i, tile(TILES), :] = weight_high
        wy[i, tile(TILES + 1), :] = beyond * next_row(beyond, beyond)
        for t, weight in ((0, weight_low), (TILES, weight_high)):
            flux = weight * gy[i, tile(t), :]
            here, there = v0[i, tile(t), :], v0[i, tile(t + 1), :]
            v0[i, tile(t), :] = jnp.where(rows == 7, here - flux, here)
            v0[i, tile(t + 1), :] = jnp.where(rows == 0, there + pltpu.roll(flux, 1, 0), there)
        totals = first_pass(i, [(0, 1), (8, 9)]) + second_pass(i, [(1, 2), (7, 9)])
        totals.append(energy(v2, wx, wy, i, (1, 2, 6, 7, 8)))
        row = jnp.zeros((1, 128), jnp.float32)
        for n, total in enumerate(totals):
            total = jnp.sum(sums[i, n] + total, axis=0, keepdims=True)
            row = jnp.where(lane == n, jnp.sum(total, axis=1, keepdims=True), row)
        moments[pair, s, pl.ds(i - PAIR * pair, 1), :] = row

    for pair in range(K // PAIR):

        @pl.when(s > 0)
        def _():
            for copy in upward(pair):
                copy.wait_send()
            for copy in downward(pair):
                copy.wait_recv()

        @pl.when(s < STRIPS - 1)
        def _():
            for copy in downward(pair):
                copy.wait_send()
            for copy in upward(pair):
                copy.wait_recv()

        @pl.loop(PAIR * pair, PAIR * pair + PAIR)
        def _(i):
            ends(i, pair)

        @pl.loop(1, STRIPS)
        def _(d):
            share(pair, d).start()

    def send_x(first, last, d, part):
        t, half, column = target(d)
        row = pl.multiple_of((16 + 16 * half) if part == 0 else 48 * half, 8)
        return pltpu.make_async_remote_copy(
            src_ref=x.at[first:last, pl.ds(row, 16), pl.ds(column, 128)],
            dst_ref=phases.at[pl.ds(K * g + first, last - first), 16 * part : 16 * part + 16],
            send_sem=x_send.at[part],
            recv_sem=x_recv.at[part],
            device_id=(t, s),
            device_id_type=MESH,
        )

    def send_c(d):
        return pltpu.make_async_remote_copy(
            src_ref=coef.at[K - 1],
            dst_ref=factors.at[g],
            send_sem=c_send,
            recv_sem=c_recv,
            device_id=(target(d)[0], s),
            device_id_type=MESH,
        )

    own_column = pl.multiple_of(128 * z, 128)
    own_rows = [pl.multiple_of(16 + 16 * core, 8), pl.multiple_of(48 * core, 8)]
    for pair in range(K // PAIR):
        others = moments.at[pair, 0 : STRIPS - 1]
        pltpu.make_async_copy(others, others, sum_recv.at[pair]).wait()
        total = moments[pair, 0]
        for d in range(1, STRIPS):
            total = total + moments[pair, d]
        spots = [jnp.broadcast_to(total[:, n : n + 1], (PAIR, 128)) for n in range(6)]
        weights = coefficients(spots)
        for i in range(PAIR * pair, PAIR * pair + PAIR):
            for j, c in enumerate(weights):
                coef[i, j : j + 1, :] = c[i - PAIR * pair : i - PAIR * pair + 1, :]
        if pair == K // PAIR - 1:
            coef[K - 1, 3:8, :] = jnp.zeros((5, 128), jnp.float32)

            for offset in PEERS:
                send_c(offset).start()

        @pl.loop(PAIR * pair, PAIR * pair + PAIR)
        def _(i):
            c0, c1, c2 = (coef[i, j : j + 1, 0:1] for j in range(3))
            for t in range(TILES):
                x[i, tile(t), :] = (
                    c0 * v0[i, tile(t + 1), :]
                    + c1 * v1[i, tile(t + 1), :]
                    + c2 * v2[i, tile(t + 1), :]
                )

        for offset in PEERS:
            send_x(PAIR * pair, min(PAIR * pair + PAIR, K - 1), offset, 0).start()

    for offset in PEERS:
        send_x(0, K, offset, 1).start()

    pltpu.make_async_copy(x, x_hbm, x_out).start()
    for part in range(2):
        phases[pl.ds(K * g, K), 16 * part : 16 * part + 16, :] = x[
            :, pl.ds(own_rows[part], 16), pl.ds(own_column, 128)
        ]

    pairs_in.wait()
    table = inverse_rows(pairs[...])
    for k in range(IFGS):
        spread[k] = jnp.broadcast_to(table[:, DATES + k : DATES + k + 1], (DATES, 128))

    def place(q):
        row = pl.multiple_of(own_rows[q // 2] + 8 * (q % 2), 8)
        return series_hbm.at[:, pl.ds(row, 8), pl.ds(own_column, 128)]

    def send_s(d, q):
        t = target(d)[0]
        return pltpu.make_async_remote_copy(
            src_ref=dates.at[pl.ds(OWN * t, OWN), tile(q)],
            dst_ref=place(q),
            send_sem=s_send.at[q],
            recv_sem=s_recv.at[q],
            device_id=(t, s),
            device_id_type=MESH,
        )

    def own_s(q):
        return pltpu.make_async_copy(
            dates.at[pl.ds(OWN * g, OWN), tile(q)], place(q), own_out.at[q]
        )

    middle = phases.at[0 : (K - 1) * (GROUPS - 1), 0:16]
    outer = phases.at[0 : K * (GROUPS - 1), 16:32]
    pltpu.make_async_copy(early.at[0 : GROUPS - 1], early.at[0 : GROUPS - 1], early_recv).wait()
    pltpu.make_async_copy(factors.at[0 : GROUPS - 1], factors.at[0 : GROUPS - 1], c_recv).wait()

    @pl.loop(1, GROUPS)
    def _(d):
        t = lax.rem(g + d, GROUPS)
        c0, c1, c2 = (factors[t, j : j + 1, :] for j in range(3))
        phases[K * t + K - 1, 0:16, :] = c0 * early[t, 0] + c1 * early[t, 1] + c2 * early[t, 2]

    for q in range(CHUNKS):
        if q == 0:
            pltpu.make_async_copy(middle, middle, x_recv.at[0]).wait()
        if q == 2:
            pltpu.make_async_copy(outer, outer, x_recv.at[1]).wait()

        def add(k, totals):
            phase = phases[k, tile(q), :]
            return tuple(
                total + spread[k, d : d + 1, :] * phase for d, total in enumerate(totals)
            )

        totals = lax.fori_loop(0, IFGS, add, (jnp.zeros((8, 128), jnp.float32),) * DATES)
        for d in range(DATES):
            dates[d, tile(q), :] = totals[d]

        for offset in PEERS:
            send_s(offset, q).start()

        own_s(q).start()

    for pair in range(K // PAIR):
        others = moments.at[pair, 0 : STRIPS - 1]
        pltpu.make_async_copy(others, others, sum_send.at[pair]).wait()
    pltpu.make_async_copy(x, x_hbm, x_out).wait()
    pltpu.make_async_copy(early.at[0 : GROUPS - 1], early.at[0 : GROUPS - 1], early_send).wait()
    pltpu.make_async_copy(factors.at[0 : GROUPS - 1], factors.at[0 : GROUPS - 1], c_send).wait()
    pltpu.make_async_copy(middle, middle, x_send.at[0]).wait()
    pltpu.make_async_copy(outer, outer, x_send.at[1]).wait()
    for q in range(CHUNKS):
        others = dates.at[0 : OWN * (GROUPS - 1), tile(q)]
        pltpu.make_async_copy(others, others, s_send.at[q]).wait()
        pltpu.make_async_copy(others, others, s_recv.at[q]).wait()
        own_s(q).wait()


def hand_over(x_ref, series_ref, x_out, series_out, sem):
    copies = [pltpu.make_async_copy(x_ref.at[i], x_out.at[i], sem.at[i]) for i in range(K)]
    copies += [
        pltpu.make_async_copy(series_ref.at[i], series_out.at[i], sem.at[K + i]) for i in range(OWN)
    ]
    for copy in copies:
        copy.start()
    for copy in copies:
        copy.wait()


def on_device(grad_x, grad_y, coherence, pairs):
    f32 = jnp.float32
    dma = pltpu.SemaphoreType.DMA
    halo = pltpu.VMEM((K, ROWS + 16, COLS), f32)
    phases, series = pl.pallas_call(
        kernel,
        out_shape=(
            jax.ShapeDtypeStruct((K, ROWS, COLS), f32),
            jax.ShapeDtypeStruct((OWN, ROWS, COLS), f32),
        ),
        in_specs=[pl.BlockSpec(memory_space=pltpu.HBM)] * 4,
        out_specs=(pl.BlockSpec(memory_space=pl.ANY),) * 2,
        scratch_shapes=[
            pltpu.VMEM((K, ROWS, COLS), f32),
            halo, halo, halo, halo,
            pltpu.VMEM((3, K, ROWS + 16, COLS), f32),
            pltpu.VMEM((K, ROWS, COLS), f32),
            pltpu.VMEM((K, 6, 8, 128), f32),
            pltpu.VMEM((K // PAIR, STRIPS, PAIR, 128), f32),
            pltpu.VMEM((K, 8, 128), f32),
            pltpu.VMEM((IFGS, DATES, 128), f32),
            pltpu.VMEM((IFGS, 32, 128), f32),
            pltpu.VMEM((GROUPS, 3, 16, 128), f32),
            pltpu.VMEM((GROUPS, 8, 128), f32),
            pltpu.VMEM((DATES, 32, 128), f32),
            pltpu.VMEM((2, IFGS), jnp.int32),
            dma((3, 3)), dma((K // PAIR, 5)), dma((K // PAIR, 5)), dma((K // PAIR,)), dma((K // PAIR,)),
            dma, dma, dma, dma,
            dma((2,)), dma((2,)), dma((CHUNKS,)), dma((CHUNKS,)), dma, dma((CHUNKS,)), dma,
        ],
        compiler_params=pltpu.CompilerParams(
            collective_id=0, has_side_effects=True, vmem_limit_bytes=52 * 1024 * 1024
        ),
    )(grad_x, grad_y, coherence, pairs.T)
    return pl.pallas_call(
        hand_over,
        out_shape=(
            jax.ShapeDtypeStruct((K, ROWS, COLS), f32),
            jax.ShapeDtypeStruct((OWN, ROWS, COLS), f32),
        ),
        in_specs=[pl.BlockSpec(memory_space=pltpu.VMEM)] * 2,
        out_specs=(pl.BlockSpec(memory_space=pl.ANY),) * 2,
        scratch_shapes=[dma((K + OWN,))],
        compiler_params=pltpu.CompilerParams(vmem_limit_bytes=4 * 1024 * 1024),
    )(phases, series)


def solution(mesh):
    split = P("ifg", "strip", None)
    return jax.shard_map(
        on_device, mesh=mesh, in_specs=(split, split, split, P()), out_specs=(split, split),
        check_vma=False,
    )
```

```python
import jax
import jax.numpy as jnp
from jax import lax
from jax.experimental import pallas as pl
from jax.experimental.pallas import tpu as pltpu
from jax.sharding import PartitionSpec as P

MESH = pl.DeviceIdType.MESH
DAMPING = 0.1
DATES = 32
IFGS = 64
GROUPS = 16
STRIPS = 16
K = 4
BATCHES = ((0, 1), (1, 2), (2, 4))
OWN = 2
ROWS = 64
COLS = 1024
TILES = ROWS // 8
CHUNKS = 4
EPS = 3e-7
EARLY = (16, 8)
OTHERS = [(dz, 1) for dz in (4, 3, 5, 2, 6, 1, 7, 0)]
STRIP_PEERS = [(dy, dx) for dy in (2, 1, 3, 0) for dx in (2, 1, 3, 0) if (dy, dx) != (0, 0)]
PEERS = [(dz, other) for dz in (4, 3, 5, 2, 6, 1, 7) for other in (0, 1)] + [(0, 1)]


def tile(t):
    return slice(8 * t, 8 * t + 8)


def rows_iota():
    return lax.broadcasted_iota(jnp.int32, (8, COLS), 0)


def fold(field):
    total = field[:, :128]
    for c in range(1, COLS // 128):
        total = total + field[:, 128 * c : 128 * c + 128]
    return total


def next_row(now, after):
    return jnp.where(rows_iota() == 7, pltpu.roll(after, 7, 0), pltpu.roll(now, 7, 0))


def edge_x(coherence):
    lanes = lax.broadcasted_iota(jnp.int32, (8, COLS), 1)
    return jnp.where(lanes == COLS - 1, 0.0, coherence * pltpu.roll(coherence, COLS - 1, 1))


def laplace(p_ref, q_ref, wx_ref, wy_ref, i, first, last, inner):
    top = rows_iota() == 0
    now = p_ref[i, tile(first), :]
    if first > 0:
        before = p_ref[i, tile(first - 1), :]
        carry = pltpu.roll(wy_ref[i, tile(first - 1), :] * (next_row(before, now) - before), 1, 0)
    else:
        carry = jnp.zeros((8, COLS), jnp.float32)
    for t in range(first, last + 1):
        after = p_ref[i, tile(t + 1), :] if t < TILES + 1 else now
        flux_y = wy_ref[i, tile(t), :] * (next_row(now, after) - now)
        flux_x = wx_ref[i, tile(t), :] * (pltpu.roll(now, COLS - 1, 1) - now)
        turned = pltpu.roll(flux_y, 1, 0)
        out = pltpu.roll(flux_x, 1, 1) - flux_x + jnp.where(top, carry, turned) - flux_y
        q_ref[i, tile(t), :] = out
        inner(t, now, out)
        carry = turned
        now = after


def energy(p_ref, wx_ref, wy_ref, i, tiles):
    total = jnp.zeros((8, 128), jnp.float32)
    for t in tiles:
        now = p_ref[i, tile(t), :]
        diff_y = next_row(now, p_ref[i, tile(t + 1), :]) - now
        diff_x = pltpu.roll(now, COLS - 1, 1) - now
        total = total + fold(
            wy_ref[i, tile(t), :] * diff_y * diff_y + wx_ref[i, tile(t), :] * diff_x * diff_x
        )
    return total


def coefficients(m):
    a = [m[j + 1] + DAMPING * m[j] for j in range(5)]
    zero = jnp.zeros_like(m[0])
    d0 = a[0]
    good0 = d0 > 0.0
    inv0 = 1.0 / jnp.where(good0, d0, 1.0)
    l1 = a[1] * inv0
    l2 = a[2] * inv0
    d1 = a[2] - l1 * a[1]
    good1 = d1 > EPS * a[2]
    inv1 = jnp.where(good1, 1.0 / jnp.where(good1, d1, 1.0), zero)
    l3 = (a[3] - l2 * a[1]) * inv1
    d2 = a[4] - l2 * a[2] - l3 * (a[3] - l2 * a[1])
    good2 = good1 & (d2 > EPS * a[4])
    inv2 = jnp.where(good2, 1.0 / jnp.where(good2, d2, 1.0), zero)
    y1 = m[1] - l1 * m[0]
    y2 = m[2] - l2 * m[0] - l3 * y1
    c2 = y2 * inv2
    c1 = y1 * inv1 - l3 * c2
    c0 = m[0] * inv0 - l1 * c1 - l2 * c2
    return c0, c1, c2


def inverse_rows(pairs):
    date = lax.broadcasted_iota(jnp.int32, (128, IFGS), 0)
    design = (pairs[1:2, :] == date).astype(jnp.float32) - (pairs[0:1, :] == date).astype(jnp.float32)
    lanes = lax.broadcasted_iota(jnp.int32, (IFGS, 128), 1)
    shifted = lanes - DATES == lax.broadcasted_iota(jnp.int32, (IFGS, 128), 0)
    table = lax.dot_general(
        design[:DATES], design, (((1,), (1,)), ((), ())), precision=lax.Precision.HIGHEST,
        preferred_element_type=jnp.float32,
    ) + jnp.dot(
        design[:DATES], shifted.astype(jnp.float32), precision=lax.Precision.HIGHEST,
        preferred_element_type=jnp.float32,
    )
    spread = lax.broadcasted_iota(jnp.int32, (DATES, 128), 1)
    level = lax.broadcasted_iota(jnp.int32, (DATES, 1), 0)
    table = table + (spread < DATES).astype(jnp.float32)
    for j in range(DATES):
        row = table[j : j + 1, :] / table[j : j + 1, j : j + 1]
        column = table[:, j : j + 1] - (level == j).astype(jnp.float32)
        table = table - column * row
    return table


def kernel(
    gx_hbm, gy_hbm, co_hbm, pairs_hbm, x_hbm, series_hbm,
    gx, gy, co, wx, wy, basis, x, sums, moments, coef, spread, phases, early, factors, dates, pairs,
    load_sem, halo_send, halo_recv, sum_send, sum_recv, early_send, early_recv, c_send, c_recv,
    x_send, x_recv, s_send, s_recv, x_out, own_out, pairs_sem,
):
    g, s = lax.axis_index("ifg"), lax.axis_index("strip")
    z, core = g // 2, lax.rem(g, 2)
    rows = rows_iota()
    lane = lax.broadcasted_iota(jnp.int32, (1, 128), 1)
    v0, v1, v2 = (basis.at[j] for j in range(3))

    def load(n, a):
        src, dst, low = ((co_hbm, co, 8), (gy_hbm, gy, 8), (gx_hbm, gx, 0))[a]
        first, last = ((0, 16), (48, 64), (16, 48))[n]
        return pltpu.make_async_copy(
            src.at[:, first:last], dst.at[:, low + first : low + last], load_sem.at[n, a]
        )

    for n in range(3):
        for a in range(3):
            load(n, a).start()
    pairs_in = pltpu.make_async_copy(pairs_hbm, pairs, pairs_sem)
    pairs_in.start()

    barrier = pltpu.get_barrier_semaphore()

    def beside(offset):
        dy, dx = offset
        return g, 4 * lax.rem(s // 4 + dy, 4) + lax.rem(lax.rem(s, 4) + dx, 4)

    def behind(offset):
        dz, other = offset
        return 2 * lax.rem(z + dz, GROUPS // 2) + lax.rem(core + other, 2), s

    for offset in PEERS:
        pl.semaphore_signal(barrier, inc=1, device_id=behind(offset), device_id_type=MESH)
    for offset in STRIP_PEERS:
        pl.semaphore_signal(barrier, inc=1, device_id=beside(offset), device_id_type=MESH)

    nothing = jnp.zeros((K, 8, COLS), jnp.float32)

    @pl.when(s == 0)
    def _():
        co[:, tile(0), :] = nothing
        gy[:, tile(0), :] = nothing
        v0[:, tile(0), :] = nothing

    @pl.when(s == STRIPS - 1)
    def _():
        co[:, tile(TILES + 1), :] = nothing
        v0[:, tile(TILES + 1), :] = nothing

    def right_side(i, first, last):
        now = co[i, tile(first), :]
        if first > 1:
            before = co[i, tile(first - 1), :]
            carry = pltpu.roll(before * next_row(before, now) * gy[i, tile(first - 1), :], 1, 0)
        else:
            carry = jnp.zeros((8, COLS), jnp.float32)
        for t in range(first, last + 1):
            after = co[i, tile(t + 1), :] if t < TILES else jnp.zeros((8, COLS), jnp.float32)
            weight_x = edge_x(now)
            weight_y = now * next_row(now, after)
            flux_x = weight_x * gx[i, tile(t - 1), :]
            flux_y = weight_y * gy[i, tile(t), :]
            turned = pltpu.roll(flux_y, 1, 0)
            wx[i, tile(t), :] = weight_x
            wy[i, tile(t), :] = weight_y
            v0[i, tile(t), :] = (
                pltpu.roll(flux_x, 1, 1) - flux_x + jnp.where(rows == 0, carry, turned) - flux_y
            )
            carry = turned
            now = after

    for n in range(2):
        for a in range(3):
            load(n, a).wait()

    @pl.loop(0, K)
    def _(i):
        right_side(i, 1, 1)
        right_side(i, TILES, TILES)

    pl.semaphore_wait(barrier, STRIPS + GROUPS - 2)

    up = jnp.maximum(s - 1, 0)
    down = jnp.minimum(s + 1, STRIPS - 1)

    def halo(i, n, src, low, high, shift, device):
        return pltpu.make_async_remote_copy(
            src_ref=src.at[slice(*BATCHES[i]), low:high],
            dst_ref=src.at[slice(*BATCHES[i]), low + shift : high + shift],
            send_sem=halo_send.at[i, n],
            recv_sem=halo_recv.at[i, n],
            device_id=(g, device),
            device_id_type=MESH,
        )

    def upward(i):
        return [halo(i, 0, co, 8, 11, ROWS, up), halo(i, 1, v0, 8, 11, ROWS, up)]

    def downward(i):
        return [
            halo(i, 2, co, 6 + ROWS, 8 + ROWS, -ROWS, down),
            halo(i, 3, v0, 6 + ROWS, 8 + ROWS, -ROWS, down),
            halo(i, 4, gy, 7 + ROWS, 8 + ROWS, -ROWS, down),
        ]

    for i in range(len(BATCHES)):

        @pl.when(s > 0)
        def _():
            for copy in upward(i):
                copy.start()

        @pl.when(s < STRIPS - 1)
        def _():
            for copy in downward(i):
                copy.start()

    def first_pass(i, spans):
        totals = [jnp.zeros((8, 128), jnp.float32)] * 3

        def inner(t, p, q):
            if 1 <= t <= TILES:
                for n, product in enumerate((p * p, p * q, q * q)):
                    totals[n] = totals[n] + fold(product)

        for low, high in spans:
            laplace(v0, v1, wx, wy, i, low, high, inner)
        return totals

    def second_pass(i, spans):
        totals = [jnp.zeros((8, 128), jnp.float32)] * 2

        def inner(t, p, q):
            if 1 <= t <= TILES:
                for n, product in enumerate((p * q, q * q)):
                    totals[n] = totals[n] + fold(product)

        for low, high in spans:
            laplace(v1, v2, wx, wy, i, low, high, inner)
        return totals

    def interior(i):
        totals = first_pass(i, [(2, 7)]) + second_pass(i, [(3, 6)])
        totals.append(energy(v2, wx, wy, i, range(3, 6)))
        for n, total in enumerate(totals):
            sums[i, n] = total

    def target(offset):
        dz, other = offset
        there, half = lax.rem(z + dz, GROUPS // 2), lax.rem(core + other, 2)
        return 2 * there + half, half, pl.multiple_of(128 * there, 128)

    def send_early(d):
        t, half, column = target(d)
        row = pl.multiple_of(8 + 16 + 16 * half, 8)
        return pltpu.make_async_remote_copy(
            src_ref=basis.at[:, K - 1, pl.ds(row, EARLY[offset[1]]), pl.ds(column, 128)],
            dst_ref=early.at[g, :, 0 : EARLY[offset[1]]],
            send_sem=early_send.at[offset[1]],
            recv_sem=early_recv.at[offset[1]],
            device_id=(t, s),
            device_id_type=MESH,
        )

    for a in range(3):
        load(2, a).wait()
    right_side(K - 1, 2, TILES - 1)
    interior(K - 1)

    for offset in PEERS:
        send_early(offset).start()

    def share(i, offset):
        return pltpu.make_async_remote_copy(
            src_ref=moments.at[i, s],
            dst_ref=moments.at[i, s],
            send_sem=sum_send.at[i],
            recv_sem=sum_recv.at[i],
            device_id=beside(offset),
            device_id_type=MESH,
        )

    def ends(i, batch):
        low, high, beyond = co[i, tile(0), :], co[i, tile(TILES), :], co[i, tile(TILES + 1), :]
        wx[i, tile(0), :] = edge_x(low)
        wx[i, tile(TILES + 1), :] = edge_x(beyond)
        weight_low = low * next_row(low, co[i, tile(1), :])
        weight_high = high * next_row(high, beyond)
        wy[i, tile(0), :] = weight_low
        wy[i, tile(TILES), :] = weight_high
        wy[i, tile(TILES + 1), :] = beyond * next_row(beyond, beyond)
        for t, weight in ((0, weight_low), (TILES, weight_high)):
            flux = weight * gy[i, tile(t), :]
            here, there = v0[i, tile(t), :], v0[i, tile(t + 1), :]
            v0[i, tile(t), :] = jnp.where(rows == 7, here - flux, here)
            v0[i, tile(t + 1), :] = jnp.where(rows == 0, there + pltpu.roll(flux, 1, 0), there)
        totals = first_pass(i, [(0, 1), (8, 9)]) + second_pass(i, [(1, 2), (7, 9)])
        totals.append(energy(v2, wx, wy, i, (1, 2, 6, 7, 8)))
        row = jnp.zeros((1, 128), jnp.float32)
        for n, total in enumerate(totals):
            total = jnp.sum(sums[i, n] + total, axis=0, keepdims=True)
            row = jnp.where(lane == n, jnp.sum(total, axis=1, keepdims=True), row)
        moments[batch, s, pl.ds(i - BATCHES[batch][0], 1), :] = row

    for batch in range(len(BATCHES)):

        @pl.loop(BATCHES[batch][0], min(BATCHES[batch][1], K - 1))
        def _(i):
            right_side(i, 2, TILES - 1)
            interior(i)

        @pl.when(s > 0)
        def _():
            for copy in upward(batch):
                copy.wait_send()
            for copy in downward(batch):
                copy.wait_recv()

        @pl.when(s < STRIPS - 1)
        def _():
            for copy in downward(batch):
                copy.wait_send()
            for copy in upward(batch):
                copy.wait_recv()

        @pl.loop(*BATCHES[batch])
        def _(i):
            ends(i, batch)

        for offset in STRIP_PEERS:
            share(batch, offset).start()

    def send_x(first, last, d, part):
        t, half, column = target(d)
        row = pl.multiple_of((16 + 16 * half) if part == 0 else 48 * half, 8)
        return pltpu.make_async_remote_copy(
            src_ref=x.at[first:last, pl.ds(row, 16), pl.ds(column, 128)],
            dst_ref=phases.at[pl.ds(K * g + first, last - first), 16 * part : 16 * part + 16],
            send_sem=x_send.at[part],
            recv_sem=x_recv.at[part],
            device_id=(t, s),
            device_id_type=MESH,
        )

    def send_rest(offset):
        t, half, column = target(offset)
        row = pl.multiple_of(24 + 16 * half, 8)
        return pltpu.make_async_remote_copy(
            src_ref=x.at[K - 1 : K, pl.ds(row, 8), pl.ds(column, 128)],
            dst_ref=phases.at[pl.ds(K * g + K - 1, 1), 8:16],
            send_sem=x_send.at[2],
            recv_sem=x_recv.at[2],
            device_id=(t, s),
            device_id_type=MESH,
        )

    def send_c(d):
        return pltpu.make_async_remote_copy(
            src_ref=coef.at[K - 1],
            dst_ref=factors.at[g],
            send_sem=c_send,
            recv_sem=c_recv,
            device_id=(target(d)[0], s),
            device_id_type=MESH,
        )

    def phase(i):
        c0, c1, c2 = (coef[i, j : j + 1, 0:1] for j in range(3))
        for t in range(TILES):
            x[i, tile(t), :] = (
                c0 * v0[i, tile(t + 1), :]
                + c1 * v1[i, tile(t + 1), :]
                + c2 * v2[i, tile(t + 1), :]
            )

    own_column = pl.multiple_of(128 * z, 128)
    own_rows = [pl.multiple_of(16 + 16 * core, 8), pl.multiple_of(48 * core, 8)]
    for batch in range(len(BATCHES)):
        others = moments.at[batch, 0 : STRIPS - 1]
        pltpu.make_async_copy(others, others, sum_recv.at[batch]).wait()
        total = moments[batch, 0]
        for d in range(1, STRIPS):
            total = total + moments[batch, d]
        spots = [jnp.broadcast_to(total[:, n : n + 1], total.shape) for n in range(6)]
        weights = coefficients(spots)
        first, last = BATCHES[batch]
        for i in range(first, last):
            for j, c in enumerate(weights):
                coef[i, j : j + 1, :] = c[i - first : i - first + 1, :]

        @pl.loop(first, min(last, K - 1))
        def _(i):
            phase(i)

        for offset in PEERS:
            send_x(first, min(last, K - 1), offset, 0).start()

    coef[K - 1, 3:8, :] = jnp.zeros((5, 128), jnp.float32)
    for offset in PEERS:
        send_c(offset).start()
    phase(K - 1)
    for offset in OTHERS:
        send_rest(offset).start()
    for offset in PEERS:
        send_x(0, K, offset, 1).start()

    pltpu.make_async_copy(x, x_hbm, x_out).start()
    for part in range(2):
        phases[pl.ds(K * g, K), 16 * part : 16 * part + 16, :] = x[
            :, pl.ds(own_rows[part], 16), pl.ds(own_column, 128)
        ]

    pairs_in.wait()
    table = inverse_rows(pairs[...])
    for k in range(IFGS):
        spread[k] = jnp.broadcast_to(table[:, DATES + k : DATES + k + 1], (DATES, 128))

    def place(q):
        row = pl.multiple_of(own_rows[q // 2] + 8 * (q % 2), 8)
        return series_hbm.at[:, pl.ds(row, 8), pl.ds(own_column, 128)]

    def send_s(d, q):
        t = target(d)[0]
        return pltpu.make_async_remote_copy(
            src_ref=dates.at[pl.ds(OWN * t, OWN), tile(q)],
            dst_ref=place(q),
            send_sem=s_send.at[q],
            recv_sem=s_recv.at[q],
            device_id=(t, s),
            device_id_type=MESH,
        )

    def own_s(q):
        return pltpu.make_async_copy(
            dates.at[pl.ds(OWN * g, OWN), tile(q)], place(q), own_out.at[q]
        )

    middle = phases.at[0 : (K - 1) * (GROUPS - 1), 0:16]
    outer = phases.at[0 : K * (GROUPS - 1), 16:32]
    halves = (early.at[0 : GROUPS // 2 - 1, :, 0 : EARLY[0]], early.at[0 : GROUPS // 2, :, 0 : EARLY[1]])
    rest = phases.at[0 : GROUPS // 2, 8:16]
    for other in range(2):
        pltpu.make_async_copy(halves[other], halves[other], early_recv.at[other]).wait()
    pltpu.make_async_copy(factors.at[0 : GROUPS - 1], factors.at[0 : GROUPS - 1], c_recv).wait()

    for offset in PEERS:
        t, count = target(offset)[0], EARLY[offset[1]]
        c0, c1, c2 = (factors[t, j : j + 1, :] for j in range(3))
        e0, e1, e2 = (early[t, j, 0:count, :] for j in range(3))
        phases[K * t + K - 1, 0:count, :] = c0 * e0 + c1 * e1 + c2 * e2

    for q in range(CHUNKS):
        if q == 0:
            pltpu.make_async_copy(middle, middle, x_recv.at[0]).wait()
        if q == 1:
            pltpu.make_async_copy(rest, rest, x_recv.at[2]).wait()
        if q == 2:
            pltpu.make_async_copy(outer, outer, x_recv.at[1]).wait()

        def add(k, totals):
            phase = phases[k, tile(q), :]
            return tuple(
                total + spread[k, d : d + 1, :] * phase for d, total in enumerate(totals)
            )

        totals = lax.fori_loop(0, IFGS, add, (jnp.zeros((8, 128), jnp.float32),) * DATES)
        for d in range(DATES):
            dates[d, tile(q), :] = totals[d]

        for offset in PEERS:
            send_s(offset, q).start()

        own_s(q).start()

    for batch in range(len(BATCHES)):
        others = moments.at[batch, 0 : STRIPS - 1]
        pltpu.make_async_copy(others, others, sum_send.at[batch]).wait()
    pltpu.make_async_copy(x, x_hbm, x_out).wait()
    for other in range(2):
        pltpu.make_async_copy(halves[other], halves[other], early_send.at[other]).wait()
    pltpu.make_async_copy(rest, rest, x_send.at[2]).wait()
    pltpu.make_async_copy(factors.at[0 : GROUPS - 1], factors.at[0 : GROUPS - 1], c_send).wait()
    pltpu.make_async_copy(middle, middle, x_send.at[0]).wait()
    pltpu.make_async_copy(outer, outer, x_send.at[1]).wait()
    for q in range(CHUNKS):
        others = dates.at[0 : OWN * (GROUPS - 1), tile(q)]
        pltpu.make_async_copy(others, others, s_send.at[q]).wait()
        pltpu.make_async_copy(others, others, s_recv.at[q]).wait()
        own_s(q).wait()


def hand_over(x_ref, series_ref, x_out, series_out, sem):
    copies = [pltpu.make_async_copy(x_ref.at[i], x_out.at[i], sem.at[i]) for i in range(K)]
    copies += [
        pltpu.make_async_copy(series_ref.at[i], series_out.at[i], sem.at[K + i]) for i in range(OWN)
    ]
    for copy in copies:
        copy.start()
    for copy in copies:
        copy.wait()


def on_device(grad_x, grad_y, coherence, pairs):
    f32 = jnp.float32
    dma = pltpu.SemaphoreType.DMA
    halo = pltpu.VMEM((K, ROWS + 16, COLS), f32)
    phases, series = pl.pallas_call(
        kernel,
        out_shape=(
            jax.ShapeDtypeStruct((K, ROWS, COLS), f32),
            jax.ShapeDtypeStruct((OWN, ROWS, COLS), f32),
        ),
        in_specs=[pl.BlockSpec(memory_space=pltpu.HBM)] * 4,
        out_specs=(pl.BlockSpec(memory_space=pl.ANY),) * 2,
        scratch_shapes=[
            pltpu.VMEM((K, ROWS, COLS), f32),
            halo, halo, halo, halo,
            pltpu.VMEM((3, K, ROWS + 16, COLS), f32),
            pltpu.VMEM((K, ROWS, COLS), f32),
            pltpu.VMEM((K, 6, 8, 128), f32),
            pltpu.VMEM((len(BATCHES), STRIPS, K, 128), f32),
            pltpu.VMEM((K, 8, 128), f32),
            pltpu.VMEM((IFGS, DATES, 128), f32),
            pltpu.VMEM((IFGS, 32, 128), f32),
            pltpu.VMEM((GROUPS, 3, 16, 128), f32),
            pltpu.VMEM((GROUPS, 8, 128), f32),
            pltpu.VMEM((DATES, 32, 128), f32),
            pltpu.VMEM((2, IFGS), jnp.int32),
            dma((3, 3)), dma((len(BATCHES), 5)), dma((len(BATCHES), 5)), dma((len(BATCHES),)), dma((len(BATCHES),)),
            dma((2,)), dma((2,)), dma, dma,
            dma((3,)), dma((3,)), dma((CHUNKS,)), dma((CHUNKS,)), dma, dma((CHUNKS,)), dma,
        ],
        compiler_params=pltpu.CompilerParams(
            collective_id=0, has_side_effects=True, vmem_limit_bytes=52 * 1024 * 1024
        ),
    )(grad_x, grad_y, coherence, pairs.T)
    return pl.pallas_call(
        hand_over,
        out_shape=(
            jax.ShapeDtypeStruct((K, ROWS, COLS), f32),
            jax.ShapeDtypeStruct((OWN, ROWS, COLS), f32),
        ),
        in_specs=[pl.BlockSpec(memory_space=pltpu.VMEM)] * 2,
        out_specs=(pl.BlockSpec(memory_space=pl.ANY),) * 2,
        scratch_shapes=[dma((K + OWN,))],
        compiler_params=pltpu.CompilerParams(vmem_limit_bytes=4 * 1024 * 1024),
    )(phases, series)


def solution(mesh):
    split = P("ifg", "strip", None)
    return jax.shard_map(
        on_device, mesh=mesh, in_specs=(split, split, split, P()), out_specs=(split, split),
        check_vma=False,
    )
```

```python
import jax
import jax.numpy as jnp
from jax import lax
from jax.experimental import pallas as pl
from jax.experimental.pallas import tpu as pltpu
from jax.sharding import PartitionSpec as P

MESH = pl.DeviceIdType.MESH
DAMPING = 0.1
DATES = 32
IFGS = 64
GROUPS = 16
STRIPS = 16
K = 4
BATCHES = ((0, 1), (1, 2), (2, 4))
OWN = 2
ROWS = 64
COLS = 1024
TILES = ROWS // 8
CHUNKS = 4
EPS = 3e-7
EARLY = (16, 8)
OTHERS = [(dz, 1) for dz in (4, 3, 5, 2, 6, 1, 7, 0)]
STRIP_PEERS = [(dy, dx) for dy in (2, 1, 3, 0) for dx in (2, 1, 3, 0) if (dy, dx) != (0, 0)]
PEERS = [(dz, other) for dz in (4, 3, 5, 2, 6, 1, 7) for other in (0, 1)] + [(0, 1)]


def tile(t):
    return slice(8 * t, 8 * t + 8)


def rows_iota():
    return lax.broadcasted_iota(jnp.int32, (8, COLS), 0)


def fold(field):
    total = field[:, :128]
    for c in range(1, COLS // 128):
        total = total + field[:, 128 * c : 128 * c + 128]
    return total


def next_row(now, after):
    return jnp.where(rows_iota() == 7, pltpu.roll(after, 7, 0), pltpu.roll(now, 7, 0))


def edge_x(coherence):
    lanes = lax.broadcasted_iota(jnp.int32, (8, COLS), 1)
    return jnp.where(lanes == COLS - 1, 0.0, coherence * pltpu.roll(coherence, COLS - 1, 1))


def laplace(p_ref, q_ref, wx_ref, wy_ref, i, first, last, inner):
    top = rows_iota() == 0
    now = p_ref[i, tile(first), :]
    if first > 0:
        before = p_ref[i, tile(first - 1), :]
        carry = pltpu.roll(wy_ref[i, tile(first - 1), :] * (next_row(before, now) - before), 1, 0)
    else:
        carry = jnp.zeros((8, COLS), jnp.float32)
    for t in range(first, last + 1):
        after = p_ref[i, tile(t + 1), :] if t < TILES + 1 else now
        flux_y = wy_ref[i, tile(t), :] * (next_row(now, after) - now)
        flux_x = wx_ref[i, tile(t), :] * (pltpu.roll(now, COLS - 1, 1) - now)
        turned = pltpu.roll(flux_y, 1, 0)
        out = pltpu.roll(flux_x, 1, 1) - flux_x + jnp.where(top, carry, turned) - flux_y
        q_ref[i, tile(t), :] = out
        inner(t, now, out)
        carry = turned
        now = after


def energy(p_ref, wx_ref, wy_ref, i, tiles):
    total = jnp.zeros((8, 128), jnp.float32)
    for t in tiles:
        now = p_ref[i, tile(t), :]
        diff_y = next_row(now, p_ref[i, tile(t + 1), :]) - now
        diff_x = pltpu.roll(now, COLS - 1, 1) - now
        total = total + fold(
            wy_ref[i, tile(t), :] * diff_y * diff_y + wx_ref[i, tile(t), :] * diff_x * diff_x
        )
    return total


def coefficients(m):
    a = [m[j + 1] + DAMPING * m[j] for j in range(5)]
    zero = jnp.zeros_like(m[0])
    d0 = a[0]
    good0 = d0 > 0.0
    inv0 = 1.0 / jnp.where(good0, d0, 1.0)
    l1 = a[1] * inv0
    l2 = a[2] * inv0
    d1 = a[2] - l1 * a[1]
    good1 = d1 > EPS * a[2]
    inv1 = jnp.where(good1, 1.0 / jnp.where(good1, d1, 1.0), zero)
    l3 = (a[3] - l2 * a[1]) * inv1
    d2 = a[4] - l2 * a[2] - l3 * (a[3] - l2 * a[1])
    good2 = good1 & (d2 > EPS * a[4])
    inv2 = jnp.where(good2, 1.0 / jnp.where(good2, d2, 1.0), zero)
    y1 = m[1] - l1 * m[0]
    y2 = m[2] - l2 * m[0] - l3 * y1
    c2 = y2 * inv2
    c1 = y1 * inv1 - l3 * c2
    c0 = m[0] * inv0 - l1 * c1 - l2 * c2
    return c0, c1, c2


def inverse_rows(pairs):
    date = lax.broadcasted_iota(jnp.int32, (128, IFGS), 0)
    design = (pairs[1:2, :] == date).astype(jnp.float32) - (pairs[0:1, :] == date).astype(jnp.float32)
    lanes = lax.broadcasted_iota(jnp.int32, (IFGS, 128), 1)
    shifted = lanes - DATES == lax.broadcasted_iota(jnp.int32, (IFGS, 128), 0)
    table = lax.dot_general(
        design[:DATES], design, (((1,), (1,)), ((), ())), precision=lax.Precision.HIGHEST,
        preferred_element_type=jnp.float32,
    ) + jnp.dot(
        design[:DATES], shifted.astype(jnp.float32), precision=lax.Precision.HIGHEST,
        preferred_element_type=jnp.float32,
    )
    spread = lax.broadcasted_iota(jnp.int32, (DATES, 128), 1)
    level = lax.broadcasted_iota(jnp.int32, (DATES, 1), 0)
    table = table + (spread < DATES).astype(jnp.float32)
    for j in range(DATES):
        row = table[j : j + 1, :] / table[j : j + 1, j : j + 1]
        column = table[:, j : j + 1] - (level == j).astype(jnp.float32)
        table = table - column * row
    return table


def kernel(
    gx_hbm, gy_hbm, co_hbm, pairs_hbm, x_hbm, series_hbm,
    gx, gy, co, wx, wy, basis, x, sums, moments, coef, spread, phases, early, factors, dates, pairs,
    load_sem, halo_send, halo_recv, sum_send, sum_recv, early_send, early_recv, c_send, c_recv,
    x_send, x_recv, s_send, s_recv, x_out, own_out, pairs_sem,
):
    g, s = lax.axis_index("ifg"), lax.axis_index("strip")
    z, core = g // 2, lax.rem(g, 2)
    rows = rows_iota()
    lane = lax.broadcasted_iota(jnp.int32, (1, 128), 1)
    v0, v1, v2 = (basis.at[j] for j in range(3))

    def load(n, a):
        src, dst, low = ((co_hbm, co, 8), (gy_hbm, gy, 8), (gx_hbm, gx, 0))[a]
        first, last = ((0, 16), (48, 64), (16, 48))[n]
        return pltpu.make_async_copy(
            src.at[:, first:last], dst.at[:, low + first : low + last], load_sem.at[n, a]
        )

    for n in range(3):
        for a in range(3):
            load(n, a).start()
    pairs_in = pltpu.make_async_copy(pairs_hbm, pairs, pairs_sem)
    pairs_in.start()

    barrier = pltpu.get_barrier_semaphore()

    def beside(offset):
        dy, dx = offset
        return g, 4 * lax.rem(s // 4 + dy, 4) + lax.rem(lax.rem(s, 4) + dx, 4)

    def behind(offset):
        dz, other = offset
        return 2 * lax.rem(z + dz, GROUPS // 2) + lax.rem(core + other, 2), s

    for offset in PEERS:
        pl.semaphore_signal(barrier, inc=1, device_id=behind(offset), device_id_type=MESH)
    for offset in STRIP_PEERS:
        pl.semaphore_signal(barrier, inc=1, device_id=beside(offset), device_id_type=MESH)

    nothing = jnp.zeros((K, 8, COLS), jnp.float32)

    @pl.when(s == 0)
    def _():
        co[:, tile(0), :] = nothing
        gy[:, tile(0), :] = nothing
        v0[:, tile(0), :] = nothing

    @pl.when(s == STRIPS - 1)
    def _():
        co[:, tile(TILES + 1), :] = nothing
        v0[:, tile(TILES + 1), :] = nothing

    def right_side(i, first, last):
        now = co[i, tile(first), :]
        if first > 1:
            before = co[i, tile(first - 1), :]
            carry = pltpu.roll(before * next_row(before, now) * gy[i, tile(first - 1), :], 1, 0)
        else:
            carry = jnp.zeros((8, COLS), jnp.float32)
        for t in range(first, last + 1):
            after = co[i, tile(t + 1), :] if t < TILES else jnp.zeros((8, COLS), jnp.float32)
            weight_x = edge_x(now)
            weight_y = now * next_row(now, after)
            flux_x = weight_x * gx[i, tile(t - 1), :]
            flux_y = weight_y * gy[i, tile(t), :]
            turned = pltpu.roll(flux_y, 1, 0)
            wx[i, tile(t), :] = weight_x
            wy[i, tile(t), :] = weight_y
            v0[i, tile(t), :] = (
                pltpu.roll(flux_x, 1, 1) - flux_x + jnp.where(rows == 0, carry, turned) - flux_y
            )
            carry = turned
            now = after

    for n in range(2):
        for a in range(3):
            load(n, a).wait()

    @pl.loop(0, K)
    def _(i):
        right_side(i, 1, 1)
        right_side(i, TILES, TILES)

    def first_pass(i, spans):
        totals = [jnp.zeros((8, 128), jnp.float32)] * 3

        def inner(t, p, q):
            if 1 <= t <= TILES:
                for n, product in enumerate((p * p, p * q, q * q)):
                    totals[n] = totals[n] + fold(product)

        for low, high in spans:
            laplace(v0, v1, wx, wy, i, low, high, inner)
        return totals

    def second_pass(i, spans):
        totals = [jnp.zeros((8, 128), jnp.float32)] * 2

        def inner(t, p, q):
            if 1 <= t <= TILES:
                for n, product in enumerate((p * q, q * q)):
                    totals[n] = totals[n] + fold(product)

        for low, high in spans:
            laplace(v1, v2, wx, wy, i, low, high, inner)
        return totals

    def interior(i):
        totals = first_pass(i, [(2, 7)]) + second_pass(i, [(3, 6)])
        totals.append(energy(v2, wx, wy, i, range(3, 6)))
        for n, total in enumerate(totals):
            sums[i, n] = total

    def target(offset):
        dz, other = offset
        there, half = lax.rem(z + dz, GROUPS // 2), lax.rem(core + other, 2)
        return 2 * there + half, half, pl.multiple_of(128 * there, 128)

    def send_early(d):
        t, half, column = target(d)
        row = pl.multiple_of(8 + 16 + 16 * half, 8)
        return pltpu.make_async_remote_copy(
            src_ref=basis.at[:, K - 1, pl.ds(row, EARLY[offset[1]]), pl.ds(column, 128)],
            dst_ref=early.at[g, :, 0 : EARLY[offset[1]]],
            send_sem=early_send.at[offset[1]],
            recv_sem=early_recv.at[offset[1]],
            device_id=(t, s),
            device_id_type=MESH,
        )

    for a in range(3):
        load(2, a).wait()
    right_side(K - 1, 2, TILES - 1)
    interior(K - 1)

    pl.semaphore_wait(barrier, STRIPS + GROUPS - 2)

    up = jnp.maximum(s - 1, 0)
    down = jnp.minimum(s + 1, STRIPS - 1)

    def halo(i, n, src, low, high, shift, device):
        return pltpu.make_async_remote_copy(
            src_ref=src.at[slice(*BATCHES[i]), low:high],
            dst_ref=src.at[slice(*BATCHES[i]), low + shift : high + shift],
            send_sem=halo_send.at[i, n],
            recv_sem=halo_recv.at[i, n],
            device_id=(g, device),
            device_id_type=MESH,
        )

    def upward(i):
        return [halo(i, 0, co, 8, 11, ROWS, up), halo(i, 1, v0, 8, 11, ROWS, up)]

    def downward(i):
        return [
            halo(i, 2, co, 6 + ROWS, 8 + ROWS, -ROWS, down),
            halo(i, 3, v0, 6 + ROWS, 8 + ROWS, -ROWS, down),
            halo(i, 4, gy, 7 + ROWS, 8 + ROWS, -ROWS, down),
        ]

    for i in range(len(BATCHES)):

        @pl.when(s > 0)
        def _():
            for copy in upward(i):
                copy.start()

        @pl.when(s < STRIPS - 1)
        def _():
            for copy in downward(i):
                copy.start()

    for offset in PEERS:
        send_early(offset).start()

    def share(i, offset):
        return pltpu.make_async_remote_copy(
            src_ref=moments.at[i, s],
            dst_ref=moments.at[i, s],
            send_sem=sum_send.at[i],
            recv_sem=sum_recv.at[i],
            device_id=beside(offset),
            device_id_type=MESH,
        )

    def ends(i, batch):
        low, high, beyond = co[i, tile(0), :], co[i, tile(TILES), :], co[i, tile(TILES + 1), :]
        wx[i, tile(0), :] = edge_x(low)
        wx[i, tile(TILES + 1), :] = edge_x(beyond)
        weight_low = low * next_row(low, co[i, tile(1), :])
        weight_high = high * next_row(high, beyond)
        wy[i, tile(0), :] = weight_low
        wy[i, tile(TILES), :] = weight_high
        wy[i, tile(TILES + 1), :] = beyond * next_row(beyond, beyond)
        for t, weight in ((0, weight_low), (TILES, weight_high)):
            flux = weight * gy[i, tile(t), :]
            here, there = v0[i, tile(t), :], v0[i, tile(t + 1), :]
            v0[i, tile(t), :] = jnp.where(rows == 7, here - flux, here)
            v0[i, tile(t + 1), :] = jnp.where(rows == 0, there + pltpu.roll(flux, 1, 0), there)
        totals = first_pass(i, [(0, 1), (8, 9)]) + second_pass(i, [(1, 2), (7, 9)])
        totals.append(energy(v2, wx, wy, i, (1, 2, 6, 7, 8)))
        row = jnp.zeros((1, 128), jnp.float32)
        for n, total in enumerate(totals):
            total = jnp.sum(sums[i, n] + total, axis=0, keepdims=True)
            row = jnp.where(lane == n, jnp.sum(total, axis=1, keepdims=True), row)
        moments[batch, s, pl.ds(i - BATCHES[batch][0], 1), :] = row

    for batch in range(len(BATCHES)):

        @pl.loop(BATCHES[batch][0], min(BATCHES[batch][1], K - 1))
        def _(i):
            right_side(i, 2, TILES - 1)
            interior(i)

        @pl.when(s > 0)
        def _():
            for copy in upward(batch):
                copy.wait_send()
            for copy in downward(batch):
                copy.wait_recv()

        @pl.when(s < STRIPS - 1)
        def _():
            for copy in downward(batch):
                copy.wait_send()
            for copy in upward(batch):
                copy.wait_recv()

        @pl.loop(*BATCHES[batch])
        def _(i):
            ends(i, batch)

        for offset in STRIP_PEERS:
            share(batch, offset).start()

    def send_x(first, last, d, part):
        t, half, column = target(d)
        row = pl.multiple_of((16 + 16 * half) if part == 0 else 48 * half, 8)
        return pltpu.make_async_remote_copy(
            src_ref=x.at[first:last, pl.ds(row, 16), pl.ds(column, 128)],
            dst_ref=phases.at[pl.ds(K * g + first, last - first), 16 * part : 16 * part + 16],
            send_sem=x_send.at[part],
            recv_sem=x_recv.at[part],
            device_id=(t, s),
            device_id_type=MESH,
        )

    def send_rest(offset):
        t, half, column = target(offset)
        row = pl.multiple_of(24 + 16 * half, 8)
        return pltpu.make_async_remote_copy(
            src_ref=x.at[K - 1 : K, pl.ds(row, 8), pl.ds(column, 128)],
            dst_ref=phases.at[pl.ds(K * g + K - 1, 1), 8:16],
            send_sem=x_send.at[2],
            recv_sem=x_recv.at[2],
            device_id=(t, s),
            device_id_type=MESH,
        )

    def send_c(d):
        return pltpu.make_async_remote_copy(
            src_ref=coef.at[K - 1],
            dst_ref=factors.at[g],
            send_sem=c_send,
            recv_sem=c_recv,
            device_id=(target(d)[0], s),
            device_id_type=MESH,
        )

    def phase(i):
        c0, c1, c2 = (coef[i, j : j + 1, 0:1] for j in range(3))
        for t in range(TILES):
            x[i, tile(t), :] = (
                c0 * v0[i, tile(t + 1), :]
                + c1 * v1[i, tile(t + 1), :]
                + c2 * v2[i, tile(t + 1), :]
            )

    own_column = pl.multiple_of(128 * z, 128)
    own_rows = [pl.multiple_of(16 + 16 * core, 8), pl.multiple_of(48 * core, 8)]
    for batch in range(len(BATCHES)):
        others = moments.at[batch, 0 : STRIPS - 1]
        pltpu.make_async_copy(others, others, sum_recv.at[batch]).wait()
        total = moments[batch, 0]
        for d in range(1, STRIPS):
            total = total + moments[batch, d]
        spots = [jnp.broadcast_to(total[:, n : n + 1], total.shape) for n in range(6)]
        weights = coefficients(spots)
        first, last = BATCHES[batch]
        for i in range(first, last):
            for j, c in enumerate(weights):
                coef[i, j : j + 1, :] = c[i - first : i - first + 1, :]

        @pl.loop(first, min(last, K - 1))
        def _(i):
            phase(i)

        for offset in PEERS:
            send_x(first, min(last, K - 1), offset, 0).start()

    coef[K - 1, 3:8, :] = jnp.zeros((5, 128), jnp.float32)
    for offset in PEERS:
        send_c(offset).start()
    phase(K - 1)
    for offset in OTHERS:
        send_rest(offset).start()
    for offset in PEERS:
        send_x(0, K, offset, 1).start()

    pltpu.make_async_copy(x, x_hbm, x_out).start()
    for part in range(2):
        phases[pl.ds(K * g, K), 16 * part : 16 * part + 16, :] = x[
            :, pl.ds(own_rows[part], 16), pl.ds(own_column, 128)
        ]

    pairs_in.wait()
    table = inverse_rows(pairs[...])
    for k in range(IFGS):
        spread[k] = jnp.broadcast_to(table[:, DATES + k : DATES + k + 1], (DATES, 128))

    def place(q):
        row = pl.multiple_of(own_rows[q // 2] + 8 * (q % 2), 8)
        return series_hbm.at[:, pl.ds(row, 8), pl.ds(own_column, 128)]

    def send_s(d, q):
        t = target(d)[0]
        return pltpu.make_async_remote_copy(
            src_ref=dates.at[pl.ds(OWN * t, OWN), tile(q)],
            dst_ref=place(q),
            send_sem=s_send.at[q],
            recv_sem=s_recv.at[q],
            device_id=(t, s),
            device_id_type=MESH,
        )

    def own_s(q):
        return pltpu.make_async_copy(
            dates.at[pl.ds(OWN * g, OWN), tile(q)], place(q), own_out.at[q]
        )

    middle = phases.at[0 : (K - 1) * (GROUPS - 1), 0:16]
    outer = phases.at[0 : K * (GROUPS - 1), 16:32]
    halves = (early.at[0 : GROUPS // 2 - 1, :, 0 : EARLY[0]], early.at[0 : GROUPS // 2, :, 0 : EARLY[1]])
    rest = phases.at[0 : GROUPS // 2, 8:16]
    for other in range(2):
        pltpu.make_async_copy(halves[other], halves[other], early_recv.at[other]).wait()
    pltpu.make_async_copy(factors.at[0 : GROUPS - 1], factors.at[0 : GROUPS - 1], c_recv).wait()

    for offset in PEERS:
        t, count = target(offset)[0], EARLY[offset[1]]
        c0, c1, c2 = (factors[t, j : j + 1, :] for j in range(3))
        e0, e1, e2 = (early[t, j, 0:count, :] for j in range(3))
        phases[K * t + K - 1, 0:count, :] = c0 * e0 + c1 * e1 + c2 * e2

    for q in range(CHUNKS):
        if q == 0:
            pltpu.make_async_copy(middle, middle, x_recv.at[0]).wait()
        if q == 1:
            pltpu.make_async_copy(rest, rest, x_recv.at[2]).wait()
        if q == 2:
            pltpu.make_async_copy(outer, outer, x_recv.at[1]).wait()

        def add(k, totals):
            phase = phases[k, tile(q), :]
            return tuple(
                total + spread[k, d : d + 1, :] * phase for d, total in enumerate(totals)
            )

        totals = lax.fori_loop(0, IFGS, add, (jnp.zeros((8, 128), jnp.float32),) * DATES)
        for d in range(DATES):
            dates[d, tile(q), :] = totals[d]

        for offset in PEERS:
            send_s(offset, q).start()

        own_s(q).start()

    for batch in range(len(BATCHES)):
        others = moments.at[batch, 0 : STRIPS - 1]
        pltpu.make_async_copy(others, others, sum_send.at[batch]).wait()
    pltpu.make_async_copy(x, x_hbm, x_out).wait()
    for other in range(2):
        pltpu.make_async_copy(halves[other], halves[other], early_send.at[other]).wait()
    pltpu.make_async_copy(rest, rest, x_send.at[2]).wait()
    pltpu.make_async_copy(factors.at[0 : GROUPS - 1], factors.at[0 : GROUPS - 1], c_send).wait()
    pltpu.make_async_copy(middle, middle, x_send.at[0]).wait()
    pltpu.make_async_copy(outer, outer, x_send.at[1]).wait()
    for q in range(CHUNKS):
        others = dates.at[0 : OWN * (GROUPS - 1), tile(q)]
        pltpu.make_async_copy(others, others, s_send.at[q]).wait()
        pltpu.make_async_copy(others, others, s_recv.at[q]).wait()
        own_s(q).wait()


def hand_over(x_ref, series_ref, x_out, series_out, sem):
    copies = [pltpu.make_async_copy(x_ref.at[i], x_out.at[i], sem.at[i]) for i in range(K)]
    copies += [
        pltpu.make_async_copy(series_ref.at[i], series_out.at[i], sem.at[K + i]) for i in range(OWN)
    ]
    for copy in copies:
        copy.start()
    for copy in copies:
        copy.wait()


def on_device(grad_x, grad_y, coherence, pairs):
    f32 = jnp.float32
    dma = pltpu.SemaphoreType.DMA
    halo = pltpu.VMEM((K, ROWS + 16, COLS), f32)
    phases, series = pl.pallas_call(
        kernel,
        out_shape=(
            jax.ShapeDtypeStruct((K, ROWS, COLS), f32),
            jax.ShapeDtypeStruct((OWN, ROWS, COLS), f32),
        ),
        in_specs=[pl.BlockSpec(memory_space=pltpu.HBM)] * 4,
        out_specs=(pl.BlockSpec(memory_space=pl.ANY),) * 2,
        scratch_shapes=[
            pltpu.VMEM((K, ROWS, COLS), f32),
            halo, halo, halo, halo,
            pltpu.VMEM((3, K, ROWS + 16, COLS), f32),
            pltpu.VMEM((K, ROWS, COLS), f32),
            pltpu.VMEM((K, 6, 8, 128), f32),
            pltpu.VMEM((len(BATCHES), STRIPS, K, 128), f32),
            pltpu.VMEM((K, 8, 128), f32),
            pltpu.VMEM((IFGS, DATES, 128), f32),
            pltpu.VMEM((IFGS, 32, 128), f32),
            pltpu.VMEM((GROUPS, 3, 16, 128), f32),
            pltpu.VMEM((GROUPS, 8, 128), f32),
            pltpu.VMEM((DATES, 32, 128), f32),
            pltpu.VMEM((2, IFGS), jnp.int32),
            dma((3, 3)), dma((len(BATCHES), 5)), dma((len(BATCHES), 5)), dma((len(BATCHES),)), dma((len(BATCHES),)),
            dma((2,)), dma((2,)), dma, dma,
            dma((3,)), dma((3,)), dma((CHUNKS,)), dma((CHUNKS,)), dma, dma((CHUNKS,)), dma,
        ],
        compiler_params=pltpu.CompilerParams(
            collective_id=0, has_side_effects=True, vmem_limit_bytes=52 * 1024 * 1024
        ),
    )(grad_x, grad_y, coherence, pairs.T)
    return pl.pallas_call(
        hand_over,
        out_shape=(
            jax.ShapeDtypeStruct((K, ROWS, COLS), f32),
            jax.ShapeDtypeStruct((OWN, ROWS, COLS), f32),
        ),
        in_specs=[pl.BlockSpec(memory_space=pltpu.VMEM)] * 2,
        out_specs=(pl.BlockSpec(memory_space=pl.ANY),) * 2,
        scratch_shapes=[dma((K + OWN,))],
        compiler_params=pltpu.CompilerParams(vmem_limit_bytes=4 * 1024 * 1024),
    )(phases, series)


def solution(mesh):
    split = P("ifg", "strip", None)
    return jax.shard_map(
        on_device, mesh=mesh, in_specs=(split, split, split, P()), out_specs=(split, split),
        check_vma=False,
    )
```
